32 devices in a mesh: clus: 8 (over z, x), tgt: 4 (over y, core).
Axes of the slice: x: 2, y: 2, z: 4, core: 2. Of those that a mesh axis runs over, the one named last changes fastest.
Arguments:
- src_pos: float32 [3, 65536], P(None, ('clus', 'tgt')), may hold values from 0 to 1
- src_weight: float32 [65536], P(('clus', 'tgt')), may hold values from 0.1 to 1
- src_pot: float32 [65536], P(('clus', 'tgt')), may hold values from -0.1 to 0.05
- src_count: int32 [256], P(('clus', 'tgt')), may hold values from 128 to 256, as said below
- tgt_pos: float32 [3, 65536], P(None, ('clus', 'tgt')), may hold values from 0 to 1
- tgt_weight: float32 [65536], P(('clus', 'tgt')), may hold values from 0.1 to 1
- tgt_pot: float32 [65536], P(('clus', 'tgt')), may hold values from -0.1 to 0.05
- tgt_count: int32 [256], P(('clus', 'tgt')), may hold values from 128 to 256, as said below
- requests: int32 [256, 2], P(('clus', 'tgt')), may hold values from 0 to 7, as said below
- pair_src: int32 [1024], P(('clus', 'tgt')), may hold values from 0 to 31, as said below
- pair_slot: int32 [1024], P(('clus', 'tgt')), may hold values from 0 to 15, as said below
- pair_count: int32 [32], P(('clus', 'tgt')), may hold values from 16 to 32, as said below
Outputs:
- grad_src_pos: float32 [3, 65536], P(None, ('clus', 'tgt'))
- grad_src_weight: float32 [65536], P(('clus', 'tgt'))
- grad_tgt_pos: float32 [3, 65536], P(None, ('clus', 'tgt'))
- grad_tgt_weight: float32 [65536], P(('clus', 'tgt'))
The draws below stay inside these ranges and needn't reach their ends.
Inputs may be any that keep to these rules, and one draw needn't show every extreme that they name: `src_count`: counts of live points, the rest of each block is padding; some block is full and some is half full. `tgt_count`: counts of live points, the rest of each block is padding; some block is full and some is half full. `requests`: each row holds 2 different local block numbers of one owner: row r of group d names blocks of the owner with clus index r and the tgt index of d. `pair_src`: source block within the group's 32 source blocks of its clus index, all tgt indices in order. `pair_slot`: slot r * 2 + m of the group's request rows; the live entries of a group name every one of its 16 slots. `pair_count`: entries past the count are padding with valid numbers and must not count.
All inputs are finite; a program needn't handle non-finite values.
Results may differ from the reference program's by a relative error of at most 0.0003.
Values sent between devices are 32-bit elements; how exact they have to be, the bound alone decides.
No kernel may reach another device: no remote copies, remote signals or barrier semaphores. Data moves between devices by JAX's collectives and lax.ppermute only.
A program may use at most 64 MiB of HBM per device.

```python
import math
import jax
import jax.numpy as jnp
from jax import lax

BLK = 256
TB_DEV = 8
REQ = 2
DEV_COUNT = 32
SB_GROUP = 32
SLOTS = 16
PAIRS_DEV = 32
NSB = 256
NTB = 256
NS = 65536
NT = 65536
N_CLUS = 8
N_TGT = 4


def block_counts(key, total):
    counts = jax.random.randint(key, (total,), BLK // 2, BLK + 1, dtype=jnp.int32)
    return counts.at[0].set(BLK).at[1].set(BLK // 2)


def draw_src_count(key, part):
    return block_counts(jax.random.fold_in(key, 11), NSB)


def draw_tgt_count(key, part):
    return block_counts(jax.random.fold_in(key, 12), NTB)


def pick_row(row_key):
    return jax.random.permutation(row_key, TB_DEV)[:REQ].astype(jnp.int32)


def draw_requests(key, part):
    row_keys = jax.random.split(jax.random.fold_in(key, 13), DEV_COUNT * N_CLUS)
    picks = jax.vmap(pick_row)(row_keys)
    spread = jnp.arange(REQ, dtype=jnp.int32) * (TB_DEV - 1) // (REQ - 1)
    return picks.at[0].set(spread)


def slot_perm(row_key):
    return jax.random.permutation(row_key, SLOTS).astype(jnp.int32)


def pair_table(key):
    base = jax.random.fold_in(key, 17)
    first_key, step_key, slot_key, order_key = jax.random.split(base, 4)
    first = jax.random.randint(first_key, (DEV_COUNT, SLOTS), 0, SB_GROUP, dtype=jnp.int32)
    first = first.at[0, 0].set(0).at[0, 1].set(SB_GROUP - 1)
    offset = jax.random.randint(step_key, (DEV_COUNT, SLOTS), 1, SB_GROUP, dtype=jnp.int32)
    second = (first + offset) % SB_GROUP
    slot_order = jax.vmap(slot_perm)(jax.random.split(slot_key, DEV_COUNT))
    shuffle = jax.vmap(slot_perm)(jax.random.split(order_key, DEV_COUNT))
    second_src = jnp.take_along_axis(second, shuffle, 1)
    second_slot = jnp.take_along_axis(slot_order, shuffle, 1)
    sources = jnp.concatenate([first, second_src], 1).reshape(-1)
    slots = jnp.concatenate([slot_order, second_slot], 1).reshape(-1)
    return (sources.astype(jnp.int32), slots.astype(jnp.int32))


def draw_pair_src(key, part):
    return pair_table(key)[0]


def draw_pair_slot(key, part):
    return pair_table(key)[1]


def draw_pair_count(key, part):
    counts = jax.random.randint(jax.random.fold_in(key, 19), (DEV_COUNT,), SLOTS, PAIRS_DEV + 1, dtype=jnp.int32)
    return counts.at[0].set(PAIRS_DEV).at[1].set(SLOTS)


def levels(key, extent, cuts, smallest, top_value):
    def one(dim, shards_of):
        steps = jax.random.uniform(jax.random.fold_in(jax.random.fold_in(key, 6), dim), (shards_of,), jnp.float32, smallest / len(cuts), top_value / len(cuts))
        return jnp.repeat(jnp.exp(steps), extent[dim] // shards_of).reshape((-1,) + (1,) * (len(extent) - dim - 1))

    gain = one(*cuts[0])
    for cut in cuts[1:]:
        gain = gain * one(*cut)
    return gain


def setup_inputs(seed: int = 0) -> dict:
    streams_of = jax.random.split(jax.random.key(seed), 13)
    return {
        "src_pos": jnp.clip(1.0 * jax.random.uniform(streams_of[0], (3, NS), jnp.float32) ** levels(streams_of[0], (3, NS), ((1, 32),), -0.2, 0.2), 0.0, 1.0),
        "src_weight": jnp.clip(jnp.exp(math.log(1.0) - 2.3025851 * jax.random.uniform(streams_of[1], (NS,), jnp.float32) ** levels(streams_of[1], (NS,), ((0, 32),), -0.2, 0.2)), 0.1, 1.0),
        "src_pot": jnp.clip(-0.1 + 0.15 * jax.random.uniform(streams_of[2], (NS,), jnp.float32) ** levels(streams_of[2], (NS,), ((0, 32),), -0.2, 0.2), -0.1, 0.05),
        "src_count": draw_src_count(jax.random.fold_in(streams_of[12], 71), 0),
        "tgt_pos": jnp.clip(1.0 * jax.random.uniform(streams_of[4], (3, NT), jnp.float32) ** levels(streams_of[4], (3, NT), ((1, 32),), -0.2, 0.2), 0.0, 1.0),
        "tgt_weight": jnp.clip(jnp.exp(math.log(1.0) - 2.3025851 * jax.random.uniform(streams_of[5], (NT,), jnp.float32) ** levels(streams_of[5], (NT,), ((0, 32),), -0.2, 0.2)), 0.1, 1.0),
        "tgt_pot": jnp.clip(-0.1 + 0.15 * jax.random.uniform(streams_of[6], (NT,), jnp.float32) ** levels(streams_of[6], (NT,), ((0, 32),), -0.2, 0.2), -0.1, 0.05),
        "tgt_count": draw_tgt_count(jax.random.fold_in(streams_of[12], 71), 0),
        "requests": draw_requests(jax.random.fold_in(streams_of[12], 71), 0),
        "pair_src": draw_pair_src(jax.random.fold_in(streams_of[12], 71), 0),
        "pair_slot": draw_pair_slot(jax.random.fold_in(streams_of[12], 71), 0),
        "pair_count": draw_pair_count(jax.random.fold_in(streams_of[12], 71), 0),
    }


entropic = 0.05
highest = lax.Precision.HIGHEST


def local_pack(positions, weights, potentials, counts):
    block_count = counts.shape[0]
    block_len = positions.shape[1] // block_count
    offsets = jnp.arange(block_len, dtype=jnp.int32)[None, :]
    live_mask = (offsets < counts[:, None]).astype(jnp.float32).reshape(-1)
    packed = jnp.concatenate([positions, (weights * live_mask)[None, :], potentials[None, :]], 0)
    return packed, live_mask


def tile_kernel(src_tiles, tgt_tiles, live_mask):
    crossed = jnp.einsum("cpi,cpj->pij", src_tiles[:3], tgt_tiles[:3], precision=highest)
    left_part = src_tiles[4] - 0.5 * jnp.sum(src_tiles[:3] * src_tiles[:3], 0)
    right_part = tgt_tiles[4] - 0.5 * jnp.sum(tgt_tiles[:3] * tgt_tiles[:3], 0)
    expo = (left_part[:, :, None] + right_part[:, None, :] + crossed) / entropic
    return jnp.exp(expo) * live_mask[:, None, None]


def source_terms(kernel, src_tiles, tgt_tiles):
    weighted = kernel * tgt_tiles[3][:, None, :]
    row_totals = jnp.sum(weighted, 2)
    shifted = jnp.einsum("pij,cpj->cpi", weighted, tgt_tiles[:3], precision=highest)
    motion = src_tiles[3][None] * (src_tiles[:3] * row_totals[None] - shifted)
    return jnp.concatenate([motion, (-entropic * row_totals)[None]], 0)


def target_terms(kernel, src_tiles, tgt_tiles):
    weighted = kernel * src_tiles[3][:, :, None]
    col_totals = jnp.sum(weighted, 1)
    shifted = jnp.einsum("pij,cpi->cpj", weighted, src_tiles[:3], precision=highest)
    motion = tgt_tiles[3][None] * (tgt_tiles[:3] * col_totals[None] - shifted)
    return jnp.concatenate([motion, (-entropic * col_totals)[None]], 0)


def reference(src_pos, src_weight, src_pot, src_count, tgt_pos, tgt_weight, tgt_pot, tgt_count, requests, pair_src, pair_slot, pair_count):
    src_packed, src_live = local_pack(src_pos, src_weight, src_pot, src_count)
    tgt_packed, tgt_live = local_pack(tgt_pos, tgt_weight, tgt_pot, tgt_count)
    src_blocks = src_packed.reshape(5, NSB, BLK)
    tgt_blocks = tgt_packed.reshape(5, NTB, BLK)
    device_ids = jnp.arange(DEV_COUNT, dtype=jnp.int32)
    slabs = requests.reshape(DEV_COUNT, N_CLUS, REQ)

    def one_device(carry, inputs):
        src_acc, tgt_acc = carry
        device, sources, slots, live_pairs, slab = inputs
        clus_idx = device // N_TGT
        tgt_idx = device % N_TGT
        src_index = (clus_idx * SB_GROUP + sources).astype(jnp.int32)
        peers = slots // REQ
        ranks = slots % REQ
        tgt_index = ((peers * N_TGT + tgt_idx) * TB_DEV + slab[peers, ranks]).astype(jnp.int32)
        live_mask = (jnp.arange(PAIRS_DEV, dtype=jnp.int32) < live_pairs).astype(jnp.float32)
        src_tiles = jnp.take(src_blocks, src_index, axis=1)
        tgt_tiles = jnp.take(tgt_blocks, tgt_index, axis=1)
        kernel = tile_kernel(src_tiles, tgt_tiles, live_mask)
        src_acc = src_acc.at[:, src_index, :].add(source_terms(kernel, src_tiles, tgt_tiles))
        tgt_acc = tgt_acc.at[:, tgt_index, :].add(target_terms(kernel, src_tiles, tgt_tiles))
        return (src_acc, tgt_acc), None

    start = (jnp.zeros((4, NSB, BLK), jnp.float32), jnp.zeros((4, NTB, BLK), jnp.float32))
    scanned = (device_ids, pair_src.reshape(DEV_COUNT, PAIRS_DEV), pair_slot.reshape(DEV_COUNT, PAIRS_DEV), pair_count, slabs)
    (src_acc, tgt_acc), _ = lax.scan(one_device, start, scanned)
    src_sums = src_acc.reshape(4, NS)
    tgt_sums = tgt_acc.reshape(4, NT)
    grad_src_pos = src_sums[:3] * src_live[None, :]
    grad_src_weight = (src_pot + src_sums[3]) * src_live
    grad_tgt_pos = tgt_sums[:3] * tgt_live[None, :]
    grad_tgt_weight = (tgt_pot + tgt_sums[3]) * tgt_live
    return grad_src_pos, grad_src_weight, grad_tgt_pos, grad_tgt_weight
```

```python
import functools
import math

import jax
import jax.numpy as jnp
from jax import lax
from jax.experimental import pallas as pl
from jax.experimental.pallas import tpu as pltpu
from jax.sharding import PartitionSpec as P

BLK = 256
LANES = 128
GROUP = 2

entropic = 0.05
LOG2E = math.log2(math.e)
SCALE = LOG2E / entropic
DEAD = -4096.0

VMEM = pl.BlockSpec(memory_space=pltpu.VMEM)
SMEM = pl.BlockSpec(memory_space=pltpu.SMEM)


def partner(i, k, n):
    return i ^ k if n & (n - 1) == 0 else (i + k) % n


def origin(i, k, n):
    return i ^ k if n & (n - 1) == 0 else (i + n - k) % n


def shifted(x, axis, k):
    n = lax.axis_size(axis)
    return lax.ppermute(x, axis, [(i, partner(i, k, n)) for i in range(n)])


def live_row(count_ref, block):
    lane = lax.broadcasted_iota(jnp.int32, (1, BLK), 1)
    return lane < count_ref[block]


def pack_side(pos_ref, weight_ref, pot_ref, count_ref, out_ref):
    for b in range(count_ref.shape[0]):
        cols = slice(b * BLK, (b + 1) * BLK)
        pos = pos_ref[:, cols]
        norm = jnp.sum(pos * pos, axis=0, keepdims=True)
        expo = (pot_ref[:, cols] - 0.5 * norm) * SCALE + jnp.log(weight_ref[:, cols]) * LOG2E
        out_ref[0:3, cols] = pos
        out_ref[3:4, cols] = jnp.where(live_row(count_ref, b), expo, DEAD)


def pack_kernel(req_ref, sc_ref, tc_ref, sp_ref, sw_ref, so_ref, tp_ref, tw_ref, to_ref, src_ref, tgt_ref):
    pack_side(sp_ref, sw_ref, so_ref, sc_ref, src_ref)
    pack_side(tp_ref, tw_ref, to_ref, tc_ref, tgt_ref)
    rows, per = req_ref.shape
    own = tp_ref.shape[1]
    width = tgt_ref.shape[1] - own
    lane = lax.broadcasted_iota(jnp.int32, (4, width), 1)
    ids = jnp.zeros((4, width), jnp.float32)
    for r in range(rows):
        for m in range(per):
            ids = jnp.where(lane == r * per + m, req_ref[r, m].astype(jnp.float32), ids)
    tgt_ref[:, own:] = ids


def split3(x):
    high = x.astype(jnp.bfloat16).astype(jnp.float32)
    rest = x - high
    mid = rest.astype(jnp.bfloat16).astype(jnp.float32)
    return high, mid, rest - mid


def main_kernel(n_tgt, n_clus, me_ref, req_ref, ps_ref, pq_ref, pc_ref, *refs):
    src_in, refs = refs[:n_tgt], refs[n_tgt:]
    tgt_in, refs = refs[:n_clus], refs[n_clus:]
    src_out, refs = refs[:n_tgt], refs[n_tgt:]
    tgt_out, refs = refs[:n_clus], refs[n_clus:]
    left, right, src_rows, tgt_rows, src_acc, tgt_acc = refs
    tgt_me, clus_me = me_ref[0], me_ref[1]
    per_dev = src_in[0].shape[1] // BLK
    n_src = n_tgt * per_dev
    per_req = req_ref.shape[1]
    last = lax.broadcasted_iota(jnp.int32, (4, BLK), 0) == 3
    pad = jnp.zeros((8, BLK), jnp.float32)

    for k in range(n_tgt):
        base = origin(tgt_me, k, n_tgt) * per_dev
        for b in range(per_dev):
            high, mid, low = split3(src_in[k][:, b * BLK : (b + 1) * BLK])
            high1, mid1 = jnp.where(last, 1.0, high), jnp.where(last, 1.0, mid)
            left[base + b] = jnp.concatenate([high, high1, high1, mid, mid1, low, pad], 0).astype(jnp.bfloat16)
            src_rows[base + b] = jnp.concatenate([high1, jnp.where(last, 0.0, mid)], 0)
    dead = lax.broadcasted_iota(jnp.int32, (32, BLK), 0) == 3
    left[n_src] = jnp.where(dead, DEAD, 0.0).astype(jnp.bfloat16)
    src_rows[n_src] = pad
    src_acc[...] = jnp.zeros_like(src_acc)
    tgt_acc[...] = jnp.zeros_like(tgt_acc)

    for k in range(n_clus):
        owner = origin(clus_me, k, n_clus)
        for m in range(per_req):
            block = req_ref[owner, m]
            raw = tgt_in[k][:, pl.ds(pl.multiple_of(block * BLK, BLK), BLK)]
            high, mid, _ = split3(raw)
            tgt_rows[owner * per_req + m] = jnp.concatenate(
                [jnp.where(last, 1.0, high), jnp.where(last, 0.0, mid)], 0
            )
            high, mid, low = split3(jnp.where(last, raw, raw * SCALE))
            high1 = jnp.where(last, 1.0, high)
            wide = jnp.concatenate([high1, mid, low, high1, jnp.where(last, high, mid), high1, pad], 0)
            right[owner * per_req + m] = wide.T.astype(jnp.bfloat16)

    count = pc_ref[0]

    def one_pair(pair):
        inside = jnp.minimum(pair, ps_ref.shape[0] - 1)
        s = jnp.where(pair < count, ps_ref[inside], n_src)
        q = pq_ref[inside]
        expo = jnp.dot(right[q], left[s], preferred_element_type=jnp.float32)
        kern = jnp.exp2(expo)
        high = kern.astype(jnp.bfloat16)
        low = (kern - high.astype(jnp.float32)).astype(jnp.bfloat16)
        y = tgt_rows[q].astype(jnp.bfloat16)
        x = src_rows[s].astype(jnp.bfloat16)
        src_part = jnp.dot(y, high, preferred_element_type=jnp.float32) + jnp.dot(
            y, low, preferred_element_type=jnp.float32
        )
        nt = (((1,), (1,)), ((), ()))
        tgt_part = lax.dot_general(x, high, nt, preferred_element_type=jnp.float32) + lax.dot_general(
            x, low, nt, preferred_element_type=jnp.float32
        )
        return s, q, src_part, tgt_part

    def body(step, carry):
        parts = [one_pair(step * GROUP + g) for g in range(GROUP)]
        for s, q, src_part, tgt_part in parts:
            src_acc[s] += src_part
            tgt_acc[q] += tgt_part
        return carry

    lax.fori_loop(0, (count + GROUP - 1) // GROUP, body, 0)

    for k in range(n_tgt):
        base = partner(tgt_me, k, n_tgt) * per_dev
        for b in range(per_dev):
            total = src_acc[base + b]
            src_out[k][:, b * BLK : (b + 1) * BLK] = total[0:4] + total[4:8]
    for k in range(n_clus):
        base = partner(clus_me, k, n_clus) * per_req
        for m in range(per_req):
            total = tgt_acc[base + m]
            tgt_out[k][:, m * BLK : (m + 1) * BLK] = total[0:4] + total[4:8]


def finish_side(pos_ref, weight_ref, pot_ref, count_ref, sums, grad_pos_ref, grad_weight_ref):
    for b in range(count_ref.shape[0]):
        cols = slice(b * BLK, (b + 1) * BLK)
        total = sums(b, cols)
        mass = total[3:4]
        live = live_row(count_ref, b)
        grad_pos_ref[:, cols] = jnp.where(live, pos_ref[:, cols] * mass - total[0:3], 0.0)
        grad_weight_ref[:, cols] = jnp.where(
            live, pot_ref[:, cols] - entropic * mass / weight_ref[:, cols], 0.0
        )


def finish_kernel(n_tgt, n_clus, per_req, me_ref, sc_ref, tc_ref, sp_ref, sw_ref, so_ref, tp_ref, tw_ref, to_ref, *refs):
    src_parts, refs = refs[:n_tgt], refs[n_tgt:]
    tgt_parts, refs = refs[:n_clus], refs[n_clus:]
    tgt_in, refs = refs[:n_clus], refs[n_clus:]
    gsp_ref, gsw_ref, gtp_ref, gtw_ref = refs
    finish_side(
        sp_ref, sw_ref, so_ref, sc_ref, lambda b, cols: sum(p[:, cols] for p in src_parts), gsp_ref, gsw_ref
    )
    clus_me = me_ref[1]
    own = tp_ref.shape[1]
    width = tgt_in[0].shape[1] - own
    lane = lax.broadcasted_iota(jnp.int32, (4, width), 1)
    ids = []
    for k in range(n_clus):
        row = tgt_in[k][:, own:]
        for m in range(per_req):
            ids.append(jnp.sum(jnp.where(lane == clus_me * per_req + m, row, 0.0), axis=1, keepdims=True))

    def tgt_sum(b, cols):
        total = jnp.zeros((4, BLK), jnp.float32)
        for k in range(n_clus):
            for m in range(per_req):
                part = tgt_parts[k][:, m * BLK : (m + 1) * BLK]
                total += jnp.where(ids[k * per_req + m] == b, part, 0.0)
        return total

    finish_side(tp_ref, tw_ref, to_ref, tc_ref, tgt_sum, gtp_ref, gtw_ref)


def shards(
    src_pos,
    src_weight,
    src_pot,
    src_count,
    tgt_pos,
    tgt_weight,
    tgt_pot,
    tgt_count,
    requests,
    pair_src,
    pair_slot,
    pair_count,
):
    f32 = jnp.float32
    n_tgt, n_clus = lax.axis_size("tgt"), lax.axis_size("clus")
    ns, nt = src_pos.shape[1], tgt_pos.shape[1]
    per_dev = ns // BLK
    per_req = requests.shape[1]
    n_src, slots = n_tgt * per_dev, n_clus * per_req
    width = -(-slots // LANES) * LANES
    params = pltpu.CompilerParams(vmem_limit_bytes=48 * 2**20)
    me = jnp.stack([lax.axis_index("tgt"), lax.axis_index("clus")]).astype(jnp.int32)
    rows = [a.reshape(1, -1) for a in (src_weight, src_pot, tgt_weight, tgt_pot)]
    points = (src_pos, rows[0], rows[1], tgt_pos, rows[2], rows[3])

    src_pack, tgt_pack = pl.pallas_call(
        pack_kernel,
        name="pack",
        out_shape=(jax.ShapeDtypeStruct((4, ns), f32), jax.ShapeDtypeStruct((4, nt + width), f32)),
        in_specs=[SMEM] * 3 + [VMEM] * 6,
        out_specs=(VMEM, VMEM),
        compiler_params=params,
    )(requests, src_count, tgt_count, *points)

    src_in = [src_pack] + [shifted(src_pack, "tgt", k) for k in range(1, n_tgt)]
    tgt_in = [tgt_pack] + [shifted(tgt_pack, "clus", k) for k in range(1, n_clus)]

    outs = pl.pallas_call(
        functools.partial(main_kernel, n_tgt, n_clus),
        name="pairs",
        out_shape=[jax.ShapeDtypeStruct((4, ns), f32)] * n_tgt
        + [jax.ShapeDtypeStruct((4, per_req * BLK), f32)] * n_clus,
        in_specs=[SMEM] * 5 + [VMEM] * (n_tgt + n_clus),
        out_specs=[VMEM] * (n_tgt + n_clus),
        scratch_shapes=[
            pltpu.VMEM((n_src + 1, 32, BLK), jnp.bfloat16),
            pltpu.VMEM((slots, BLK, 32), jnp.bfloat16),
            pltpu.VMEM((n_src + 1, 8, BLK), f32),
            pltpu.VMEM((slots, 8, BLK), f32),
            pltpu.VMEM((n_src + 1, 8, BLK), f32),
            pltpu.VMEM((slots, 8, BLK), f32),
        ],
        compiler_params=params,
    )(me, requests, pair_src, pair_slot, pair_count, *src_in, *tgt_in)
    src_out, tgt_out = outs[:n_tgt], outs[n_tgt:]

    src_parts = [src_out[0]] + [shifted(src_out[k], "tgt", k) for k in range(1, n_tgt)]
    tgt_parts = [tgt_out[0]] + [shifted(tgt_out[k], "clus", k) for k in range(1, n_clus)]

    gsp, gsw, gtp, gtw = pl.pallas_call(
        functools.partial(finish_kernel, n_tgt, n_clus, per_req),
        name="finish",
        out_shape=(
            jax.ShapeDtypeStruct((3, ns), f32),
            jax.ShapeDtypeStruct((1, ns), f32),
            jax.ShapeDtypeStruct((3, nt), f32),
            jax.ShapeDtypeStruct((1, nt), f32),
        ),
        in_specs=[SMEM] * 3 + [VMEM] * (6 + n_tgt + 2 * n_clus),
        out_specs=(VMEM,) * 4,
        compiler_params=params,
    )(me, src_count, tgt_count, *points, *src_parts, *tgt_parts, *tgt_in)
    return gsp, gsw.reshape(-1), gtp, gtw.reshape(-1)


def solution(mesh):
    placed = (
        P(None, ("clus", "tgt")),
        P(("clus", "tgt")),
        P(("clus", "tgt")),
        P(("clus", "tgt")),
        P(None, ("clus", "tgt")),
        P(("clus", "tgt")),
        P(("clus", "tgt")),
        P(("clus", "tgt")),
        P(("clus", "tgt"), None),
        P(("clus", "tgt")),
        P(("clus", "tgt")),
        P(("clus", "tgt")),
    )
    return jax.shard_map(
        shards,
        mesh=mesh,
        in_specs=placed,
        out_specs=(
            P(None, ("clus", "tgt")),
            P(("clus", "tgt")),
            P(None, ("clus", "tgt")),
            P(("clus", "tgt")),
        ),
        check_vma=False,
    )
```

```python
import functools
import math

import jax
import jax.numpy as jnp
from jax import lax
from jax.experimental import pallas as pl
from jax.experimental.pallas import tpu as pltpu
from jax.sharding import PartitionSpec as P

BLK = 256
LANES = 128
GROUP = 4

entropic = 0.05
LOG2E = math.log2(math.e)
SCALE = LOG2E / entropic
DEAD = -4096.0
PACK_VMEM = 60 * 2**20
MAIN_VMEM = 24 * 2**20

VMEM = pl.BlockSpec(memory_space=pltpu.VMEM)
SMEM = pl.BlockSpec(memory_space=pltpu.SMEM)


def step(i, k, n):
    return i ^ k if n & (n - 1) == 0 else (i + k) % n


def back(i, k, n):
    return i ^ k if n & (n - 1) == 0 else (i + n - k) % n


def split_axis(n):
    inner = 2 if n % 2 == 0 else 1
    return n // inner, inner


def moved(x, axis, k):
    n = lax.axis_size(axis)
    return lax.ppermute(x, axis, [(i, step(i, k, n)) for i in range(n)])


def moved_outer(x, axis, k):
    outer, inner = split_axis(lax.axis_size(axis))
    pairs = [(o * inner + i, step(o, k, outer) * inner + i) for o in range(outer) for i in range(inner)]
    return lax.ppermute(x, axis, pairs)


def moved_inner(x, axis, k):
    outer, inner = split_axis(lax.axis_size(axis))
    pairs = [(o * inner + i, o * inner + step(i, k, inner)) for o in range(outer) for i in range(inner)]
    return lax.ppermute(x, axis, pairs)


def live_row(count_ref, block):
    lane = lax.broadcasted_iota(jnp.int32, (1, BLK), 1)
    return lane < count_ref[block]


def pack_side(pos_ref, weight_ref, pot_ref, count_ref, out_ref):
    for b in range(count_ref.shape[0]):
        cols = slice(b * BLK, (b + 1) * BLK)
        pos = pos_ref[:, cols]
        norm = jnp.sum(pos * pos, axis=0, keepdims=True)
        expo = (pot_ref[:, cols] - 0.5 * norm) * SCALE + jnp.log(weight_ref[:, cols]) * LOG2E
        out_ref[0:3, cols] = pos
        out_ref[3:4, cols] = jnp.where(live_row(count_ref, b), expo, DEAD)


def pack_kernel(req_ref, sc_ref, tc_ref, sp_ref, sw_ref, so_ref, tp_ref, tw_ref, to_ref, src_ref, tgt_ref):
    pack_side(sp_ref, sw_ref, so_ref, sc_ref, src_ref)
    pack_side(tp_ref, tw_ref, to_ref, tc_ref, tgt_ref)
    per, rows = req_ref.shape
    own = tp_ref.shape[1]
    width = tgt_ref.shape[1] - own
    lane = lax.broadcasted_iota(jnp.int32, (4, width), 1)
    ids = jnp.zeros((4, width), jnp.float32)
    for r in range(rows):
        for m in range(per):
            ids = jnp.where(lane == r * per + m, req_ref[m, r].astype(jnp.float32), ids)
    tgt_ref[:, own:] = ids


def split3(x):
    high = x.astype(jnp.bfloat16).astype(jnp.float32)
    rest = x - high
    mid = rest.astype(jnp.bfloat16).astype(jnp.float32)
    return high, mid, rest - mid


def main_kernel(n_tgt, n_clus, me_ref, req_ref, ps_ref, pq_ref, pc_ref, *refs):
    outer, inner = split_axis(n_clus)
    src_in, refs = refs[:n_tgt], refs[n_tgt:]
    tgt_in, refs = refs[:outer], refs[outer:]
    src_out, refs = refs[:n_tgt], refs[n_tgt:]
    tgt_out, left, right, src_rows, tgt_rows, src_acc, tgt_acc, *kern_bufs = refs
    tgt_me, outer_me, inner_me = me_ref[0], me_ref[1], me_ref[2]
    per_dev = src_in[0].shape[1] // BLK
    n_src = n_tgt * per_dev
    per_req = req_ref.shape[0]
    last = lax.broadcasted_iota(jnp.int32, (4, BLK), 0) == 3
    pad = jnp.zeros((8, BLK), jnp.float32)

    for k in range(n_tgt):
        base = back(tgt_me, k, n_tgt) * per_dev
        for b in range(per_dev):
            high, mid, low = split3(src_in[k][:, b * BLK : (b + 1) * BLK])
            high1, mid1 = jnp.where(last, 1.0, high), jnp.where(last, 1.0, mid)
            left[base + b] = jnp.concatenate([high, high1, high1, mid, mid1, low, pad], 0).astype(jnp.bfloat16)
            src_rows[base + b] = jnp.concatenate([high1, jnp.where(last, 0.0, mid)], 0)
    dead = lax.broadcasted_iota(jnp.int32, (32, BLK), 0) == 3
    left[n_src] = jnp.where(dead, DEAD, 0.0).astype(jnp.bfloat16)
    src_rows[n_src] = pad
    src_acc[...] = jnp.zeros_like(src_acc)
    tgt_acc[...] = jnp.zeros_like(tgt_acc)

    for k in range(outer):
        for i in range(inner):
            owner = back(outer_me, k, outer) * inner + back(inner_me, i, inner)
            for m in range(per_req):
                block = req_ref[m, owner]
                raw = tgt_in[k][4 * i : 4 * i + 4, pl.ds(pl.multiple_of(block * BLK, BLK), BLK)]
                high, mid, _ = split3(raw)
                tgt_rows[owner * per_req + m] = jnp.concatenate(
                    [jnp.where(last, 1.0, high), jnp.where(last, 0.0, mid)], 0
                )
                high, mid, low = split3(jnp.where(last, raw, raw * SCALE))
                high1 = jnp.where(last, 1.0, high)
                wide = jnp.concatenate([high1, mid, low, high1, jnp.where(last, high, mid), high1, pad], 0)
                right[owner * per_req + m] = wide.T.astype(jnp.bfloat16)

    count = pc_ref[0]

    def pair_ids(pair):
        inside = jnp.minimum(pair, ps_ref.shape[0] - 1)
        return jnp.where(pair < count, ps_ref[inside], n_src), pq_ref[inside]

    def weigh(pair, buf, g):
        s, q = pair_ids(pair)
        kern = jnp.exp2(jnp.dot(right[q], left[s], preferred_element_type=jnp.float32))
        high = kern.astype(jnp.bfloat16)
        buf[g, 0] = high
        buf[g, 1] = (kern - high.astype(jnp.float32)).astype(jnp.bfloat16)

    def reduce(pair, buf, g):
        s, q = pair_ids(pair)
        high, low = buf[g, 0], buf[g, 1]
        y = tgt_rows[q].astype(jnp.bfloat16)
        x = src_rows[s].astype(jnp.bfloat16)
        dot = functools.partial(jnp.dot, preferred_element_type=jnp.float32)
        dot_t = functools.partial(
            lax.dot_general, dimension_numbers=(((1,), (1,)), ((), ())), preferred_element_type=jnp.float32
        )
        return s, q, dot(y, high) + dot(y, low), dot_t(x, high) + dot_t(x, low)

    bufs = len(kern_bufs)
    for g in range(GROUP):
        weigh(g, kern_bufs[0], g)

    def body(turn, carry):
        first = turn * bufs * GROUP
        for u in range(bufs):
            parts = []
            for g in range(GROUP):
                weigh(first + (u + 1) * GROUP + g, kern_bufs[(u + 1) % bufs], g)
                parts.append(reduce(first + u * GROUP + g, kern_bufs[u], g))
            for s, q, src_part, tgt_part in parts:
                src_acc[s] += src_part
                tgt_acc[q] += tgt_part
        return carry

    lax.fori_loop(0, (count + GROUP * bufs - 1) // (GROUP * bufs), body, 0)

    for k in range(n_tgt):
        base = step(tgt_me, k, n_tgt) * per_dev
        for b in range(per_dev):
            total = src_acc[base + b]
            src_out[k][:, b * BLK : (b + 1) * BLK] = total[0:4] + total[4:8]
    for r in range(n_clus):
        for m in range(per_req):
            total = tgt_acc[r * per_req + m]
            tgt_out[r, :, m * BLK : (m + 1) * BLK] = total[0:4] + total[4:8]


def finish_side(pos_ref, weight_ref, pot_ref, count_ref, sums, grad_pos_ref, grad_weight_ref):
    for b in range(count_ref.shape[0]):
        cols = slice(b * BLK, (b + 1) * BLK)
        total = sums(b, cols)
        mass = total[3:4]
        live = live_row(count_ref, b)
        grad_pos_ref[:, cols] = jnp.where(live, pos_ref[:, cols] * mass - total[0:3], 0.0)
        grad_weight_ref[:, cols] = jnp.where(
            live, pot_ref[:, cols] - entropic * mass / weight_ref[:, cols], 0.0
        )


def src_kernel(n_tgt, per_req, me_ref, count_ref, pos_ref, weight_ref, pot_ref, *refs):
    parts, refs = refs[:n_tgt], refs[n_tgt:]
    *tgt_in, grad_pos_ref, grad_weight_ref, ids_ref = refs
    finish_side(
        pos_ref,
        weight_ref,
        pot_ref,
        count_ref,
        lambda b, cols: sum(p[:, cols] for p in parts),
        grad_pos_ref,
        grad_weight_ref,
    )
    outer = len(tgt_in)
    inner = tgt_in[0].shape[0] // 4
    outer_me, inner_me = me_ref[1], me_ref[2]
    me = outer_me * inner + inner_me
    width = tgt_in[0].shape[1] - count_ref.shape[0] * BLK
    lane = lax.broadcasted_iota(jnp.int32, (1, width), 1)
    for k in range(outer):
        for i in range(inner):
            peer = back(outer_me, k, outer) * inner + back(inner_me, i, inner)
            row = tgt_in[k][4 * i : 4 * i + 1, tgt_in[k].shape[1] - width :]
            for m in range(per_req):
                block = jnp.sum(jnp.where(lane == me * per_req + m, row, 0.0), axis=1, keepdims=True)
                ids_ref[peer * per_req + m] = jnp.broadcast_to(block, (1, BLK))


def tgt_kernel(count_ref, pos_ref, weight_ref, pot_ref, parts_ref, ids_ref, grad_pos_ref, grad_weight_ref):
    per_req = parts_ref.shape[2] // BLK

    def sums(b, cols):
        total = jnp.zeros((4, BLK), jnp.float32)
        for r in range(parts_ref.shape[0]):
            for m in range(per_req):
                part = parts_ref[r, :, m * BLK : (m + 1) * BLK]
                total += jnp.where(ids_ref[r * per_req + m] == b, part, 0.0)
        return total

    finish_side(pos_ref, weight_ref, pot_ref, count_ref, sums, grad_pos_ref, grad_weight_ref)


def shards(
    src_pos,
    src_weight,
    src_pot,
    src_count,
    tgt_pos,
    tgt_weight,
    tgt_pot,
    tgt_count,
    requests,
    pair_src,
    pair_slot,
    pair_count,
):
    f32 = jnp.float32
    n_tgt, n_clus = lax.axis_size("tgt"), lax.axis_size("clus")
    outer, inner = split_axis(n_clus)
    ns, nt = src_pos.shape[1], tgt_pos.shape[1]
    n_src = n_tgt * (ns // BLK)
    per_req = requests.shape[1]
    slots = n_clus * per_req
    width = -(-slots // LANES) * LANES
    asked = requests.T
    small = pltpu.CompilerParams(vmem_limit_bytes=MAIN_VMEM)
    clus_me = lax.axis_index("clus")
    me = jnp.stack([lax.axis_index("tgt"), clus_me // inner, clus_me % inner]).astype(jnp.int32)
    src_side = (src_pos, src_weight.reshape(1, -1), src_pot.reshape(1, -1))
    tgt_side = (tgt_pos, tgt_weight.reshape(1, -1), tgt_pot.reshape(1, -1))

    src_pack, tgt_pack = pl.pallas_call(
        pack_kernel,
        name="pack",
        out_shape=(jax.ShapeDtypeStruct((4, ns), f32), jax.ShapeDtypeStruct((4, nt + width), f32)),
        in_specs=[SMEM] * 3 + [VMEM] * 6,
        out_specs=(VMEM, VMEM),
        compiler_params=pltpu.CompilerParams(vmem_limit_bytes=PACK_VMEM),
    )(asked, src_count, tgt_count, *src_side, *tgt_side)

    src_in = [src_pack] + [moved(src_pack, "tgt", k) for k in range(1, n_tgt)]
    near = jnp.concatenate([tgt_pack] + [moved_inner(tgt_pack, "clus", k) for k in range(1, inner)], 0)
    tgt_in = [near] + [moved_outer(near, "clus", k) for k in range(1, outer)]

    *src_out, tgt_out = pl.pallas_call(
        functools.partial(main_kernel, n_tgt, n_clus),
        name="pairs",
        out_shape=[jax.ShapeDtypeStruct((4, ns), f32)] * n_tgt
        + [jax.ShapeDtypeStruct((n_clus, 4, per_req * BLK), f32)],
        in_specs=[SMEM] * 5 + [VMEM] * (n_tgt + outer),
        out_specs=[VMEM] * (n_tgt + 1),
        scratch_shapes=[
            pltpu.VMEM((n_src + 1, 32, BLK), jnp.bfloat16),
            pltpu.VMEM((slots, BLK, 32), jnp.bfloat16),
            pltpu.VMEM((n_src + 1, 8, BLK), f32),
            pltpu.VMEM((slots, 8, BLK), f32),
            pltpu.VMEM((n_src + 1, 8, BLK), f32),
            pltpu.VMEM((slots, 8, BLK), f32),
            pltpu.VMEM((GROUP, 2, BLK, BLK), jnp.bfloat16),
            pltpu.VMEM((GROUP, 2, BLK, BLK), jnp.bfloat16),
        ],
        compiler_params=small,
    )(me, asked, pair_src, pair_slot, pair_count, *src_in, *tgt_in)

    src_parts = [src_out[0]] + [moved(src_out[k], "tgt", k) for k in range(1, n_tgt)]
    tgt_parts = lax.all_to_all(tgt_out, "clus", split_axis=0, concat_axis=0, tiled=True)

    grad_src_pos, grad_src_weight, ids = pl.pallas_call(
        functools.partial(src_kernel, n_tgt, per_req),
        name="finish_src",
        out_shape=(
            jax.ShapeDtypeStruct((3, ns), f32),
            jax.ShapeDtypeStruct((1, ns), f32),
            jax.ShapeDtypeStruct((slots, 1, BLK), f32),
        ),
        in_specs=[SMEM] * 2 + [VMEM] * (3 + n_tgt + outer),
        out_specs=(VMEM,) * 3,
        compiler_params=small,
    )(me, src_count, *src_side, *src_parts, *tgt_in)
    grad_tgt_pos, grad_tgt_weight = pl.pallas_call(
        tgt_kernel,
        name="finish_tgt",
        out_shape=(jax.ShapeDtypeStruct((3, nt), f32), jax.ShapeDtypeStruct((1, nt), f32)),
        in_specs=[SMEM] + [VMEM] * 5,
        out_specs=(VMEM,) * 2,
        compiler_params=small,
    )(tgt_count, *tgt_side, tgt_parts, ids)
    return grad_src_pos, grad_src_weight.reshape(-1), grad_tgt_pos, grad_tgt_weight.reshape(-1)


def solution(mesh):
    placed = (
        P(None, ("clus", "tgt")),
        P(("clus", "tgt")),
        P(("clus", "tgt")),
        P(("clus", "tgt")),
        P(None, ("clus", "tgt")),
        P(("clus", "tgt")),
        P(("clus", "tgt")),
        P(("clus", "tgt")),
        P(("clus", "tgt"), None),
        P(("clus", "tgt")),
        P(("clus", "tgt")),
        P(("clus", "tgt")),
    )
    return jax.shard_map(
        shards,
        mesh=mesh,
        in_specs=placed,
        out_specs=(
            P(None, ("clus", "tgt")),
            P(("clus", "tgt")),
            P(None, ("clus", "tgt")),
            P(("clus", "tgt")),
        ),
        check_vma=False,
    )
```

```python
import functools
import math

import jax
import jax.numpy as jnp
from jax import lax
from jax.experimental import pallas as pl
from jax.experimental.pallas import tpu as pltpu
from jax.sharding import PartitionSpec as P

BLK = 256
LANES = 128
GROUP = 2
BUFS = 4

entropic = 0.05
LOG2E = math.log2(math.e)
SCALE = LOG2E / entropic
DEAD = -4096.0
PACK_VMEM = 60 * 2**20
MAIN_VMEM = 24 * 2**20

VMEM = pl.BlockSpec(memory_space=pltpu.VMEM)
SMEM = pl.BlockSpec(memory_space=pltpu.SMEM)


def step(i, k, n):
    return i ^ k if n & (n - 1) == 0 else (i + k) % n


def back(i, k, n):
    return i ^ k if n & (n - 1) == 0 else (i + n - k) % n


def split_axis(n):
    inner = 2 if n % 2 == 0 else 1
    return n // inner, inner


def moved(x, axis, k):
    n = lax.axis_size(axis)
    return lax.ppermute(x, axis, [(i, step(i, k, n)) for i in range(n)])


def moved_outer(x, axis, k):
    outer, inner = split_axis(lax.axis_size(axis))
    pairs = [(o * inner + i, step(o, k, outer) * inner + i) for o in range(outer) for i in range(inner)]
    return lax.ppermute(x, axis, pairs)


def moved_inner(x, axis, k):
    outer, inner = split_axis(lax.axis_size(axis))
    pairs = [(o * inner + i, o * inner + step(i, k, inner)) for o in range(outer) for i in range(inner)]
    return lax.ppermute(x, axis, pairs)


def live_row(count_ref, block):
    lane = lax.broadcasted_iota(jnp.int32, (1, BLK), 1)
    return lane < count_ref[block]


def pack_side(pos_ref, weight_ref, pot_ref, count_ref, out_ref):
    for b in range(count_ref.shape[0]):
        cols = slice(b * BLK, (b + 1) * BLK)
        pos = pos_ref[:, cols]
        norm = jnp.sum(pos * pos, axis=0, keepdims=True)
        expo = (pot_ref[:, cols] - 0.5 * norm) * SCALE + jnp.log(weight_ref[:, cols]) * LOG2E
        out_ref[0:3, cols] = pos
        out_ref[3:4, cols] = jnp.where(live_row(count_ref, b), expo, DEAD)


def pack_kernel(req_ref, sc_ref, tc_ref, sp_ref, sw_ref, so_ref, tp_ref, tw_ref, to_ref, src_ref, tgt_ref):
    pack_side(sp_ref, sw_ref, so_ref, sc_ref, src_ref)
    pack_side(tp_ref, tw_ref, to_ref, tc_ref, tgt_ref)
    per, rows = req_ref.shape
    own = tp_ref.shape[1]
    width = tgt_ref.shape[1] - own
    lane = lax.broadcasted_iota(jnp.int32, (4, width), 1)
    ids = jnp.zeros((4, width), jnp.float32)
    for r in range(rows):
        for m in range(per):
            ids = jnp.where(lane == r * per + m, req_ref[m, r].astype(jnp.float32), ids)
    tgt_ref[:, own:] = ids


def split3(x):
    high = x.astype(jnp.bfloat16).astype(jnp.float32)
    rest = x - high
    mid = rest.astype(jnp.bfloat16).astype(jnp.float32)
    return high, mid, rest - mid


def stages(outer):
    cuts = sorted({0, min(1, outer), min(2, outer), outer})
    return list(zip(cuts[:-1], cuts[1:]))


def dot(x, y):
    return jnp.dot(x, y, preferred_element_type=jnp.float32)


def dot_t(x, y):
    return lax.dot_general(x, y, (((1,), (1,)), ((), ())), preferred_element_type=jnp.float32)


def prepare_src(tgt_me, src_in, left, src_rows):
    last = lax.broadcasted_iota(jnp.int32, (4, BLK), 0) == 3
    pad = jnp.zeros((8, BLK), jnp.float32)
    per_dev = src_in[0].shape[1] // BLK
    n_src = len(src_in) * per_dev
    for k in range(len(src_in)):
        base = back(tgt_me, k, len(src_in)) * per_dev
        for b in range(per_dev):
            high, mid, low = split3(src_in[k][:, b * BLK : (b + 1) * BLK])
            high1, mid1 = jnp.where(last, 1.0, high), jnp.where(last, 1.0, mid)
            left[base + b] = jnp.concatenate([high, high1, high1, mid, mid1, low, pad], 0).astype(jnp.bfloat16)
            src_rows[base + b] = jnp.concatenate([high1, jnp.where(last, 0.0, mid)], 0)
    dead = lax.broadcasted_iota(jnp.int32, (32, BLK), 0) == 3
    left[n_src] = jnp.where(dead, DEAD, 0.0).astype(jnp.bfloat16)
    src_rows[n_src] = pad


def prepare_tgt(owner, rows, req_ref, tgt_in, right, tgt_rows):
    last = lax.broadcasted_iota(jnp.int32, (4, BLK), 0) == 3
    pad = jnp.zeros((8, BLK), jnp.float32)
    per_req = req_ref.shape[0]
    for m in range(per_req):
        block = req_ref[m, owner]
        raw = tgt_in[rows, pl.ds(pl.multiple_of(block * BLK, BLK), BLK)]
        high, mid, _ = split3(raw)
        tgt_rows[owner * per_req + m] = jnp.concatenate(
            [jnp.where(last, 1.0, high), jnp.where(last, 0.0, mid)], 0
        )
        high, mid, low = split3(jnp.where(last, raw, raw * SCALE))
        high1 = jnp.where(last, 1.0, high)
        wide = jnp.concatenate([high1, mid, low, high1, jnp.where(last, high, mid), high1, pad], 0)
        right[owner * per_req + m] = wide.T.astype(jnp.bfloat16)


def pairs_kernel(n_tgt, n_clus, first, stop, me_ref, req_ref, ps_ref, pq_ref, pc_ref, *refs):
    outer, inner = split_axis(n_clus)
    per_req = req_ref.shape[0]
    begins, ends = first == 0, stop == outer
    refs = list(refs)
    take = lambda n: [refs.pop(0) for _ in range(n)]
    if begins:
        src_in = take(n_tgt)
    else:
        left, src_rows, src_sums = take(3)
    tgt_in = take(stop - first)
    if ends:
        done = take(len(stages(outer)) - 1)
        src_out, (tgt_out,) = take(n_tgt), take(1)
        (src_acc,) = take(1)
    else:
        if begins:
            left, src_rows = take(2)
        src_acc, tgt_out = take(2)
    if begins and ends:
        left, src_rows = take(2)
    right, tgt_rows, tgt_acc, chosen, *kern_bufs = refs
    tgt_me, outer_me, inner_me = me_ref[0], me_ref[1], me_ref[2]
    n_src = left.shape[0] - 1

    count = pc_ref[0]
    total = 0
    for pair in range(ps_ref.shape[0]):
        place = lax.div(pq_ref[pair], per_req * inner)
        away = (place ^ outer_me) if outer & (outer - 1) == 0 else lax.rem(outer_me - place + outer, outer)
        chosen[total] = pair
        total = total + ((pair < count) & (away >= first) & (away < stop)).astype(jnp.int32)

    if begins:
        prepare_src(tgt_me, src_in, left, src_rows)
        src_acc[...] = jnp.zeros_like(src_acc)
    else:
        src_acc[...] = src_sums[...]
    tgt_acc[...] = jnp.zeros_like(tgt_acc)
    owners = []
    for k in range(first, stop):
        for i in range(inner):
            owner = back(outer_me, k, outer) * inner + back(inner_me, i, inner)
            owners.append(owner)
            prepare_tgt(owner, slice(4 * i, 4 * i + 4), req_ref, tgt_in[k - first], right, tgt_rows)

    def pair_ids(entry):
        pair = chosen[jnp.clip(entry, 0, jnp.maximum(total - 1, 0))]
        return jnp.where(entry < total, ps_ref[pair], n_src), pq_ref[pair]

    def weigh(entry, buf, g):
        s, q = pair_ids(entry)
        q = jnp.where(entry < total, q, owners[0] * per_req)
        kern = jnp.exp2(dot(right[q], left[s]))
        high = kern.astype(jnp.bfloat16)
        buf[g, 0] = high
        buf[g, 1] = (kern - high.astype(jnp.float32)).astype(jnp.bfloat16)

    def reduce(entry, buf, g):
        s, q = pair_ids(entry)
        q = jnp.where(entry < total, q, owners[0] * per_req)
        high, low = buf[g, 0], buf[g, 1]
        y = tgt_rows[q].astype(jnp.bfloat16)
        x = src_rows[s].astype(jnp.bfloat16)
        return s, q, dot(y, high) + dot(y, low), dot_t(x, high) + dot_t(x, low)

    bufs = len(kern_bufs)
    for g in range(GROUP):
        weigh(g, kern_bufs[0], g)

    def body(turn, carry):
        start = turn * bufs * GROUP
        for u in range(bufs):
            parts = []
            for g in range(GROUP):
                weigh(start + (u + 1) * GROUP + g, kern_bufs[(u + 1) % bufs], g)
                parts.append(reduce(start + u * GROUP + g, kern_bufs[u], g))
            for s, q, src_part, tgt_part in parts:
                src_acc[s] += src_part
                tgt_acc[q] += tgt_part
        return carry

    lax.fori_loop(0, lax.div(total + GROUP * bufs - 1, GROUP * bufs), body, 0)

    for place, owner in enumerate(owners):
        row = owner if ends else place
        for m in range(per_req):
            part = tgt_acc[owner * per_req + m]
            tgt_out[row, :, m * BLK : (m + 1) * BLK] = part[0:4] + part[4:8]
    if ends:
        for (begin, end), part in zip(stages(outer), done):
            for k in range(begin, end):
                for i in range(inner):
                    owner = back(outer_me, k, outer) * inner + back(inner_me, i, inner)
                    tgt_out[owner] = part[(k - begin) * inner + i]
        per_dev = n_src // n_tgt
        for k in range(n_tgt):
            base = step(tgt_me, k, n_tgt) * per_dev
            for b in range(per_dev):
                part = src_acc[base + b]
                src_out[k][:, b * BLK : (b + 1) * BLK] = part[0:4] + part[4:8]


def finish_side(pos_ref, weight_ref, pot_ref, count_ref, sums, grad_pos_ref, grad_weight_ref):
    for b in range(count_ref.shape[0]):
        cols = slice(b * BLK, (b + 1) * BLK)
        total = sums(b, cols)
        mass = total[3:4]
        live = live_row(count_ref, b)
        grad_pos_ref[:, cols] = jnp.where(live, pos_ref[:, cols] * mass - total[0:3], 0.0)
        grad_weight_ref[:, cols] = jnp.where(
            live, pot_ref[:, cols] - entropic * mass / weight_ref[:, cols], 0.0
        )


def src_kernel(n_tgt, per_req, me_ref, count_ref, pos_ref, weight_ref, pot_ref, *refs):
    parts, refs = refs[:n_tgt], refs[n_tgt:]
    *tgt_in, grad_pos_ref, grad_weight_ref, ids_ref = refs
    finish_side(
        pos_ref,
        weight_ref,
        pot_ref,
        count_ref,
        lambda b, cols: sum(p[:, cols] for p in parts),
        grad_pos_ref,
        grad_weight_ref,
    )
    outer = len(tgt_in)
    inner = tgt_in[0].shape[0] // 4
    outer_me, inner_me = me_ref[1], me_ref[2]
    me = outer_me * inner + inner_me
    width = tgt_in[0].shape[1] - count_ref.shape[0] * BLK
    lane = lax.broadcasted_iota(jnp.int32, (1, width), 1)
    for k in range(outer):
        for i in range(inner):
            peer = back(outer_me, k, outer) * inner + back(inner_me, i, inner)
            row = tgt_in[k][4 * i : 4 * i + 1, tgt_in[k].shape[1] - width :]
            for m in range(per_req):
                block = jnp.sum(jnp.where(lane == me * per_req + m, row, 0.0), axis=1, keepdims=True)
                ids_ref[peer * per_req + m] = jnp.broadcast_to(block, (1, BLK))


def tgt_kernel(count_ref, pos_ref, weight_ref, pot_ref, parts_ref, ids_ref, grad_pos_ref, grad_weight_ref):
    per_req = parts_ref.shape[2] // BLK

    def sums(b, cols):
        total = jnp.zeros((4, BLK), jnp.float32)
        for r in range(parts_ref.shape[0]):
            for m in range(per_req):
                part = parts_ref[r, :, m * BLK : (m + 1) * BLK]
                total += jnp.where(ids_ref[r * per_req + m] == b, part, 0.0)
        return total

    finish_side(pos_ref, weight_ref, pot_ref, count_ref, sums, grad_pos_ref, grad_weight_ref)


def shards(
    src_pos,
    src_weight,
    src_pot,
    src_count,
    tgt_pos,
    tgt_weight,
    tgt_pot,
    tgt_count,
    requests,
    pair_src,
    pair_slot,
    pair_count,
):
    f32 = jnp.float32
    n_tgt, n_clus = lax.axis_size("tgt"), lax.axis_size("clus")
    outer, inner = split_axis(n_clus)
    ns, nt = src_pos.shape[1], tgt_pos.shape[1]
    n_src = n_tgt * (ns // BLK)
    per_req = requests.shape[1]
    slots = n_clus * per_req
    width = -(-slots // LANES) * LANES
    asked = requests.T
    small = pltpu.CompilerParams(vmem_limit_bytes=MAIN_VMEM)
    clus_me = lax.axis_index("clus")
    me = jnp.stack([lax.axis_index("tgt"), clus_me // inner, clus_me % inner]).astype(jnp.int32)
    src_side = (src_pos, src_weight.reshape(1, -1), src_pot.reshape(1, -1))
    tgt_side = (tgt_pos, tgt_weight.reshape(1, -1), tgt_pot.reshape(1, -1))

    src_pack, tgt_pack = pl.pallas_call(
        pack_kernel,
        name="pack",
        out_shape=(jax.ShapeDtypeStruct((4, ns), f32), jax.ShapeDtypeStruct((4, nt + width), f32)),
        in_specs=[SMEM] * 3 + [VMEM] * 6,
        out_specs=(VMEM, VMEM),
        compiler_params=pltpu.CompilerParams(vmem_limit_bytes=PACK_VMEM),
    )(asked, src_count, tgt_count, *src_side, *tgt_side)

    src_in = [src_pack] + [moved(src_pack, "tgt", k) for k in range(1, n_tgt)]
    near = jnp.concatenate([tgt_pack] + [moved_inner(tgt_pack, "clus", k) for k in range(1, inner)], 0)
    tgt_in = [near] + [moved_outer(near, "clus", k) for k in range(1, outer)]

    block_rows = jax.ShapeDtypeStruct((n_src + 1, 8, BLK), f32)
    left_side = jax.ShapeDtypeStruct((n_src + 1, 32, BLK), jnp.bfloat16)
    scratch = [
        pltpu.VMEM((slots, BLK, 32), jnp.bfloat16),
        pltpu.VMEM((slots, 8, BLK), f32),
        pltpu.VMEM((slots, 8, BLK), f32),
        pltpu.SMEM((pair_src.shape[0] + 1,), jnp.int32),
    ] + [pltpu.VMEM((GROUP, 2, BLK, BLK), jnp.bfloat16)] * BUFS
    lists = (me, asked, pair_src, pair_slot, pair_count)
    state, done = (), []
    for first, stop in stages(outer):
        begins, ends = first == 0, stop == outer
        args = (src_in if begins else list(state)) + tgt_in[first:stop] + (done if ends else [])
        outs = []
        if begins and not ends:
            outs += [left_side, block_rows]
        if ends:
            outs += [jax.ShapeDtypeStruct((4, ns), f32)] * n_tgt
            outs += [jax.ShapeDtypeStruct((n_clus, 4, per_req * BLK), f32)]
        else:
            outs += [block_rows, jax.ShapeDtypeStruct(((stop - first) * inner, 4, per_req * BLK), f32)]
        extra = [pltpu.VMEM(block_rows.shape, f32)] if ends else []
        if begins and ends:
            extra += [pltpu.VMEM(left_side.shape, jnp.bfloat16), pltpu.VMEM(block_rows.shape, f32)]
        share = pair_src.shape[0] * (stop - first) // outer
        res = pl.pallas_call(
            functools.partial(pairs_kernel, n_tgt, n_clus, first, stop),
            name=f"pairs_{first}_{stop}",
            out_shape=outs,
            in_specs=[SMEM] * 5 + [VMEM] * len(args),
            out_specs=[VMEM] * len(outs),
            scratch_shapes=extra + scratch,
            compiler_params=small,
            cost_estimate=pl.CostEstimate(
                flops=share * 10 * BLK**3, bytes_accessed=2**20, transcendentals=share * BLK**2
            ),
        )(*lists, *args)
        if ends:
            *src_out, tgt_out = res
        else:
            if begins:
                state = res[:3]
            else:
                state = (state[0], state[1], res[0])
            done = done + [res[-1]]

    src_parts = [src_out[0]] + [moved(src_out[k], "tgt", k) for k in range(1, n_tgt)]
    tgt_parts = lax.all_to_all(tgt_out, "clus", split_axis=0, concat_axis=0, tiled=True)

    grad_src_pos, grad_src_weight, ids = pl.pallas_call(
        functools.partial(src_kernel, n_tgt, per_req),
        name="finish_src",
        out_shape=(
            jax.ShapeDtypeStruct((3, ns), f32),
            jax.ShapeDtypeStruct((1, ns), f32),
            jax.ShapeDtypeStruct((slots, 1, BLK), f32),
        ),
        in_specs=[SMEM] * 2 + [VMEM] * (3 + n_tgt + outer),
        out_specs=(VMEM,) * 3,
        compiler_params=small,
    )(me, src_count, *src_side, *src_parts, *tgt_in)
    grad_tgt_pos, grad_tgt_weight = pl.pallas_call(
        tgt_kernel,
        name="finish_tgt",
        out_shape=(jax.ShapeDtypeStruct((3, nt), f32), jax.ShapeDtypeStruct((1, nt), f32)),
        in_specs=[SMEM] + [VMEM] * 5,
        out_specs=(VMEM,) * 2,
        compiler_params=small,
    )(tgt_count, *tgt_side, tgt_parts, ids)
    return grad_src_pos, grad_src_weight.reshape(-1), grad_tgt_pos, grad_tgt_weight.reshape(-1)


def solution(mesh):
    placed = (
        P(None, ("clus", "tgt")),
        P(("clus", "tgt")),
        P(("clus", "tgt")),
        P(("clus", "tgt")),
        P(None, ("clus", "tgt")),
        P(("clus", "tgt")),
        P(("clus", "tgt")),
        P(("clus", "tgt")),
        P(("clus", "tgt"), None),
        P(("clus", "tgt")),
        P(("clus", "tgt")),
        P(("clus", "tgt")),
    )
    return jax.shard_map(
        shards,
        mesh=mesh,
        in_specs=placed,
        out_specs=(
            P(None, ("clus", "tgt")),
            P(("clus", "tgt")),
            P(None, ("clus", "tgt")),
            P(("clus", "tgt")),
        ),
        check_vma=False,
    )
```

```python
import functools
import math

import jax
import jax.numpy as jnp
from jax import lax
from jax.experimental import pallas as pl
from jax.experimental.pallas import tpu as pltpu
from jax.sharding import PartitionSpec as P

BLK = 256
LANES = 128
GROUP = 2
BUFS = 4

entropic = 0.05
LOG2E = math.log2(math.e)
SCALE = LOG2E / entropic
DEAD = -4096.0
PACK_VMEM = 60 * 2**20
MAIN_VMEM = 24 * 2**20

VMEM = pl.BlockSpec(memory_space=pltpu.VMEM)
SMEM = pl.BlockSpec(memory_space=pltpu.SMEM)
ANY = pl.BlockSpec(memory_space=pl.ANY)


def divide(x, n):
    shift = n.bit_length() - 1
    return lax.shift_right_logical(x, jnp.int32(shift)) if n == 1 << shift else lax.div(x, jnp.int32(n))


def step(i, k, n):
    return i ^ k if n & (n - 1) == 0 else (i + k) % n


def back(i, k, n):
    return i ^ k if n & (n - 1) == 0 else (i + n - k) % n


def flip(k, n):
    return k if n & (n - 1) == 0 else (n - k) % n


def split_axis(n):
    inner = 2 if n % 2 == 0 else 1
    return n // inner, inner


def moved(x, axis, k):
    n = lax.axis_size(axis)
    return lax.ppermute(x, axis, [(i, step(i, k, n)) for i in range(n)])


def moved_outer(x, axis, k):
    outer, inner = split_axis(lax.axis_size(axis))
    pairs = [(o * inner + i, step(o, k, outer) * inner + i) for o in range(outer) for i in range(inner)]
    return lax.ppermute(x, axis, pairs)


def moved_inner(x, axis, k):
    outer, inner = split_axis(lax.axis_size(axis))
    pairs = [(o * inner + i, o * inner + step(i, k, inner)) for o in range(outer) for i in range(inner)]
    return lax.ppermute(x, axis, pairs)


def live_row(count_ref, block):
    lane = lax.broadcasted_iota(jnp.int32, (1, BLK), 1)
    return lane < count_ref[block]


def pack_side(pos_ref, weight_ref, pot_ref, count_ref, out_ref):
    for b in range(count_ref.shape[0]):
        cols = slice(b * BLK, (b + 1) * BLK)
        pos = pos_ref[:, cols]
        norm = jnp.sum(pos * pos, axis=0, keepdims=True)
        expo = (pot_ref[:, cols] - 0.5 * norm) * SCALE + jnp.log(weight_ref[:, cols]) * LOG2E
        out_ref[0:3, cols] = pos
        out_ref[3:4, cols] = jnp.where(live_row(count_ref, b), expo, DEAD)


def pack_kernel(
    req_ref, ps_ref, pq_ref, sc_ref, tc_ref, sp_ref, sw_ref, so_ref, tp_ref, tw_ref, to_ref, src_ref, tgt_ref, plan_ref
):
    pairs = ps_ref.shape[0]
    for pair in range(pairs):
        plan_ref[req_ref.size + pair] = ps_ref[pair]
        plan_ref[req_ref.size + pairs + pair] = pq_ref[pair]
    pack_side(sp_ref, sw_ref, so_ref, sc_ref, src_ref)
    pack_side(tp_ref, tw_ref, to_ref, tc_ref, tgt_ref)
    per, rows = req_ref.shape
    own = tp_ref.shape[1]
    width = tgt_ref.shape[1] - own
    lane = lax.broadcasted_iota(jnp.int32, (4, width), 1)
    ids = jnp.zeros((4, width), jnp.float32)
    for r in range(rows):
        for m in range(per):
            block = req_ref[m, r]
            plan_ref[r * per + m] = block
            ids = jnp.where(lane == r * per + m, block.astype(jnp.float32), ids)
    tgt_ref[:, own:] = ids


def split3(x):
    high = x.astype(jnp.bfloat16).astype(jnp.float32)
    rest = x - high
    mid = rest.astype(jnp.bfloat16).astype(jnp.float32)
    return high, mid, rest - mid


def stages(outer):
    cuts = [(0, 1), (outer - 1, outer), (1, outer - 1)]
    return [(first, stop) for i, (first, stop) in enumerate(cuts) if first < stop and (i == 0 or first > 0)]


def dot(x, y):
    return jnp.dot(x, y, preferred_element_type=jnp.float32)


def dot_t(x, y):
    return lax.dot_general(x, y, (((1,), (1,)), ((), ())), preferred_element_type=jnp.float32)


def away(i, me, n):
    return i ^ me if n & (n - 1) == 0 else lax.rem(me - i + n, n)


def is_power(n):
    return n & (n - 1) == 0


def local_block(s, me, n, per_dev):
    if is_power(n) and is_power(per_dev):
        return s ^ (me * per_dev)
    dev = divide(s, per_dev)
    return s + (away(dev, me, n) - dev) * per_dev


def local_slot(q, outer_me, inner_me, outer, inner, per_req):
    if is_power(outer) and is_power(inner) and is_power(per_req):
        return q ^ ((outer_me * inner + inner_me) * per_req)
    clus = divide(q, per_req)
    place = divide(clus, inner)
    side = away(clus - place * inner, inner_me, inner)
    return (away(place, outer_me, outer) * inner + side - clus) * per_req + q


def prepare_src(src_in, left, src_rows):
    last = lax.broadcasted_iota(jnp.int32, (4, BLK), 0) == 3
    pad = jnp.zeros((8, BLK), jnp.float32)
    per_dev = src_in[0].shape[1] // BLK
    for k, part in enumerate(src_in):
        for b in range(per_dev):
            high, mid, low = split3(part[:, b * BLK : (b + 1) * BLK])
            high1, mid1 = jnp.where(last, 1.0, high), jnp.where(last, 1.0, mid)
            place = k * per_dev + b
            left[place] = jnp.concatenate([high, high1, high1, mid, mid1, low, pad], 0).astype(jnp.bfloat16)
            src_rows[place] = jnp.concatenate([high1, jnp.where(last, 0.0, mid)], 0)
    dead = lax.broadcasted_iota(jnp.int32, (32, BLK), 0) == 3
    left[len(src_in) * per_dev] = jnp.where(dead, DEAD, 0.0).astype(jnp.bfloat16)
    src_rows[len(src_in) * per_dev] = pad


def prepare_tgt(slot, block, rows, tgt_in, right, tgt_rows):
    last = lax.broadcasted_iota(jnp.int32, (4, BLK), 0) == 3
    pad = jnp.zeros((8, BLK), jnp.float32)
    raw = tgt_in[rows, pl.ds(pl.multiple_of(block * BLK, BLK), BLK)]
    high, mid, _ = split3(raw)
    tgt_rows[slot] = jnp.concatenate([jnp.where(last, 1.0, high), jnp.where(last, 0.0, mid)], 0)
    high, mid, low = split3(jnp.where(last, raw, raw * SCALE))
    high1 = jnp.where(last, 1.0, high)
    wide = jnp.concatenate([high1, mid, low, high1, jnp.where(last, high, mid), high1, pad], 0)
    right[slot] = wide.T.astype(jnp.bfloat16)


def pairs_kernel(n_tgt, n_clus, per_req, turn, *refs):
    outer, inner = split_axis(n_clus)
    first, stop = stages(outer)[turn]
    begins, ends = turn == 0, turn == len(stages(outer)) - 1
    refs = list(refs)
    take = lambda n: [refs.pop(0) for _ in range(n)]
    far_lists = take(2)
    if begins:
        src_in = take(n_tgt)
    else:
        left, src_rows, src_sums = take(3)
    tgt_in = take(stop - first)
    held = [k for cut in stages(outer)[1:turn] for k in range(*cut)] if ends else []
    held_in = take(len(held))
    if begins and not ends:
        left, src_rows = take(2)
    src_out = take(n_tgt if ends else 1)
    tgt_out = take(stop - first)
    for far, near in zip(held_in, take(len(held))):
        near[...] = far[...]
    src_acc = take(1)[0] if ends else src_out[0]
    if begins and ends:
        left, src_rows = take(2)
    right, tgt_rows, tgt_acc, chosen_src, chosen_slot, sems, *refs = refs
    lists, kern_bufs = refs[:2], refs[2:]
    copies = [pltpu.make_async_copy(far, near, sems.at[i]) for i, (far, near) in enumerate(zip(far_lists, lists))]
    for copy in copies:
        copy.start()
    n_src = left.shape[0] - 1
    per_dev = n_src // n_tgt
    if begins:
        prepare_src(src_in, left, src_rows)
        src_acc[...] = jnp.zeros_like(src_acc)
    else:
        src_acc[...] = src_sums[...]
    tgt_acc[...] = jnp.zeros_like(tgt_acc)
    for copy in copies:
        copy.wait()

    me_ref, plan_ref = lists
    slots = n_clus * per_req
    pairs = (plan_ref.shape[0] - slots) // 2
    tgt_me, outer_me, inner_me, count = (me_ref[i] for i in range(4))
    owners = []
    for k in range(first, stop):
        for i in range(inner):
            owner = back(outer_me, k, outer) * inner + back(inner_me, i, inner)
            for m in range(per_req):
                slot = len(owners) * per_req + m
                prepare_tgt(slot, plan_ref[owner * per_req + m], slice(4 * i, 4 * i + 4), tgt_in[k - first], right, tgt_rows)
            owners.append(owner)

    total = jnp.int32(0)
    for pair in range(pairs):
        chosen_src[total] = local_block(plan_ref[slots + pair], tgt_me, n_tgt, per_dev)
        slot = local_slot(plan_ref[slots + pairs + pair], outer_me, inner_me, outer, inner, per_req) - first * inner * per_req
        chosen_slot[total] = slot
        total = total + ((pair < count) & (slot >= 0) & (slot < len(owners) * per_req)).astype(jnp.int32)

    def pair_ids(entry):
        inside = jnp.minimum(entry, pairs - 1)
        live = entry < total
        return jnp.where(live, chosen_src[inside], n_src), jnp.where(live, chosen_slot[inside], 0)

    def weigh(entry, buf, g):
        s, q = pair_ids(entry)
        kern = jnp.exp2(dot(right[q], left[s]))
        high = kern.astype(jnp.bfloat16)
        buf[g, 0] = high
        buf[g, 1] = (kern - high.astype(jnp.float32)).astype(jnp.bfloat16)

    def reduce(entry, buf, g):
        s, q = pair_ids(entry)
        high, low = buf[g, 0], buf[g, 1]
        y = tgt_rows[q].astype(jnp.bfloat16)
        x = src_rows[s].astype(jnp.bfloat16)
        return s, q, dot(y, high) + dot(y, low), dot_t(x, high) + dot_t(x, low)

    bufs = len(kern_bufs)
    for g in range(GROUP):
        weigh(g, kern_bufs[0], g)

    def body(trip, carry):
        start = trip * bufs * GROUP
        for u in range(bufs):
            parts = []
            for g in range(GROUP):
                weigh(start + (u + 1) * GROUP + g, kern_bufs[(u + 1) % bufs], g)
                parts.append(reduce(start + u * GROUP + g, kern_bufs[u], g))
            for s, q, src_part, tgt_part in parts:
                src_acc[s] += src_part
                tgt_acc[q] += tgt_part
        return carry

    lax.fori_loop(0, divide(total + GROUP * bufs - 1, GROUP * bufs), body, 0)

    for place in range(len(owners)):
        for m in range(per_req):
            part = tgt_acc[place * per_req + m]
            tgt_out[place // inner][place % inner, :, m * BLK : (m + 1) * BLK] = part[0:4] + part[4:8]
    if ends:
        for k in range(n_tgt):
            base = flip(k, n_tgt) * per_dev
            for b in range(per_dev):
                part = src_acc[base + b]
                src_out[k][:, b * BLK : (b + 1) * BLK] = part[0:4] + part[4:8]


def join_kernel(*refs):
    *parts, out_ref = refs
    for k, part in enumerate(parts):
        out_ref[4 * k : 4 * k + 4] = part[...]


def keep_kernel(*refs):
    refs[-1][...] = refs[0][...]


def pick_kernel(*refs):
    *parts, out_ref = refs
    for k, part in enumerate(parts):
        out_ref[k] = part[1]


def finish_side(pos, weight, pot, live, total):
    mass = total[3:4]
    return pos * mass - total[0:3], jnp.where(live, pot - entropic * mass / weight, 0.0)


def src_kernel(n_tgt, per_req, me_ref, src_count_ref, tgt_count_ref, pos_ref, weight_ref, pot_ref, *refs):
    parts, refs = refs[:n_tgt], refs[n_tgt:]
    *tgt_in, grad_pos_ref, grad_weight_ref, ids_ref, live_ref = refs
    for b in range(src_count_ref.shape[0]):
        cols = slice(b * BLK, (b + 1) * BLK)
        grad_pos_ref[:, cols], grad_weight_ref[:, cols] = finish_side(
            pos_ref[:, cols],
            weight_ref[:, cols],
            pot_ref[:, cols],
            live_row(src_count_ref, b),
            sum(p[:, cols] for p in parts),
        )
    for b in range(tgt_count_ref.shape[0]):
        live_ref[:, b * BLK : (b + 1) * BLK] = live_row(tgt_count_ref, b).astype(jnp.float32)
    outer = len(tgt_in)
    inner = tgt_in[0].shape[0] // 4
    outer_me, inner_me = me_ref[1], me_ref[2]
    me = outer_me * inner + inner_me
    own = tgt_count_ref.shape[0] * BLK
    width = tgt_in[0].shape[1] - own
    lane = lax.broadcasted_iota(jnp.int32, (1, width), 1)
    for k in range(outer):
        for i in range(inner):
            row = tgt_in[flip(k, outer)][4 * i : 4 * i + 1, own:]
            for m in range(per_req):
                block = jnp.sum(jnp.where(lane == me * per_req + m, row, 0.0), axis=1, keepdims=True)
                ids_ref[(k * inner + i) * per_req + m] = jnp.broadcast_to(block, (4, BLK))


def tgt_kernel(outer, inner, pos_ref, weight_ref, pot_ref, live_ref, ids_ref, *refs):
    *parts, grad_pos_ref, grad_weight_ref = refs
    own, side = parts[:outer], parts[outer:]
    per_req = ids_ref.shape[0] // (outer * inner)
    for b in range(pos_ref.shape[1] // BLK):
        cols = slice(b * BLK, (b + 1) * BLK)
        total = jnp.zeros((4, BLK), jnp.float32)
        for k in range(outer):
            for i in range(inner):
                for m in range(per_req):
                    wide = slice(m * BLK, (m + 1) * BLK)
                    part = own[k][0, :, wide] if i == 0 else side[i - 1][k, :, wide]
                    total += jnp.where(ids_ref[(k * inner + i) * per_req + m] == b, part, 0.0)
        grad_pos_ref[:, cols], grad_weight_ref[:, cols] = finish_side(
            pos_ref[:, cols], weight_ref[:, cols], pot_ref[:, cols], live_ref[:, cols] > 0.0, total
        )


def shards(
    src_pos,
    src_weight,
    src_pot,
    src_count,
    tgt_pos,
    tgt_weight,
    tgt_pot,
    tgt_count,
    requests,
    pair_src,
    pair_slot,
    pair_count,
):
    f32 = jnp.float32
    n_tgt, n_clus = lax.axis_size("tgt"), lax.axis_size("clus")
    outer, inner = split_axis(n_clus)
    ns, nt = src_pos.shape[1], tgt_pos.shape[1]
    n_src = n_tgt * (ns // BLK)
    per_req = requests.shape[1]
    slots = n_clus * per_req
    width = -(-slots // LANES) * LANES
    asked = requests.T
    small = pltpu.CompilerParams(vmem_limit_bytes=MAIN_VMEM)
    clus_me = lax.axis_index("clus")
    me = jnp.stack([lax.axis_index("tgt"), clus_me // inner, clus_me % inner, pair_count[0]]).astype(jnp.int32)
    src_side = (src_pos, src_weight.reshape(1, -1), src_pot.reshape(1, -1))
    tgt_side = (tgt_pos, tgt_weight.reshape(1, -1), tgt_pot.reshape(1, -1))

    src_pack, tgt_pack, plan = pl.pallas_call(
        pack_kernel,
        name="pack",
        out_shape=(
            jax.ShapeDtypeStruct((4, ns), f32),
            jax.ShapeDtypeStruct((4, nt + width), f32),
            jax.ShapeDtypeStruct((slots + 2 * pair_src.shape[0],), jnp.int32),
        ),
        in_specs=[SMEM] * 5 + [VMEM] * 6,
        out_specs=(VMEM, VMEM, SMEM),
        compiler_params=pltpu.CompilerParams(vmem_limit_bytes=PACK_VMEM),
    )(asked, pair_src, pair_slot, src_count, tgt_count, *src_side, *tgt_side)

    src_in = [src_pack] + [moved(src_pack, "tgt", k) for k in range(1, n_tgt)]
    near = [tgt_pack] + [moved_inner(tgt_pack, "clus", k) for k in range(1, inner)]
    near = pl.pallas_call(
        join_kernel,
        name="join",
        out_shape=jax.ShapeDtypeStruct((4 * inner, nt + width), f32),
        in_specs=[VMEM] * inner,
        out_specs=VMEM,
        compiler_params=small,
    )(*near)
    tgt_in = [near] + [moved_outer(near, "clus", k) for k in range(1, outer)]

    block_rows = jax.ShapeDtypeStruct((n_src + 1, 8, BLK), f32)
    left_side = jax.ShapeDtypeStruct((n_src + 1, 32, BLK), jnp.bfloat16)
    lists = (me, plan)
    scratch = (
        [pltpu.SMEM((pair_src.shape[0] + 1,), jnp.int32)] * 2
        + [pltpu.SemaphoreType.DMA((len(lists),))]
        + [pltpu.SMEM(a.shape, jnp.int32) for a in lists]
        + [pltpu.VMEM((GROUP, 2, BLK, BLK), jnp.bfloat16)] * BUFS
    )
    part_shape = jax.ShapeDtypeStruct((inner, 4, per_req * BLK), f32)
    state, sums = (), {}
    for turn, (first, stop) in enumerate(stages(outer)):
        begins, ends = turn == 0, turn == len(stages(outer)) - 1
        held = [k for cut in stages(outer)[1:turn] for k in range(*cut)] if ends else []
        args = (src_in if begins else list(state)) + tgt_in[first:stop] + [sums[k] for k in held]
        outs = [left_side, block_rows] if begins and not ends else []
        outs += [jax.ShapeDtypeStruct((4, ns), f32)] * n_tgt if ends else [block_rows]
        outs += [part_shape] * (stop - first + len(held))
        extra = [pltpu.VMEM(block_rows.shape, f32)] if ends else []
        if begins and ends:
            extra += [pltpu.VMEM(left_side.shape, jnp.bfloat16), pltpu.VMEM(block_rows.shape, f32)]
        near = (stop - first) * inner * per_req
        extra += [
            pltpu.VMEM((near, BLK, 32), jnp.bfloat16),
            pltpu.VMEM((near, 8, BLK), f32),
            pltpu.VMEM((near, 8, BLK), f32),
        ]
        res = pl.pallas_call(
            functools.partial(pairs_kernel, n_tgt, n_clus, per_req, turn),
            name=f"pairs_{first}_{stop}",
            out_shape=outs,
            in_specs=[ANY] * len(lists) + [VMEM] * len(args),
            out_specs=[VMEM] * len(outs),
            scratch_shapes=extra + scratch,
            compiler_params=small,
            cost_estimate=pl.CostEstimate(flops=4*10**8 if begins else 0, bytes_accessed=2**20, transcendentals=0),
        )(*lists, *args)
        made = list(range(first, stop)) + held
        sums.update(zip(made, res[len(res) - len(made) :]))
        if ends:
            src_out = res[:n_tgt]
        else:
            state = tuple(res[:3]) if begins else (state[0], state[1], res[0])

    src_parts = [src_out[0]] + [moved(src_out[k], "tgt", k) for k in range(1, n_tgt)]
    tgt_parts = [sums[0]] + [moved_outer(sums[k], "clus", flip(k, outer)) for k in range(1, outer)]
    part_keep = functools.partial(
        pl.pallas_call,
        keep_kernel,
        name="keep",
        out_shape=part_shape,
        out_specs=VMEM,
        compiler_params=small,
    )
    for k in reversed(range(2, outer)):
        late = tgt_parts[k + 1 : k + 2]
        tgt_parts[k] = part_keep(in_specs=[VMEM] * (1 + len(late)))(tgt_parts[k], *late)
    if inner == 2:
        beside = pl.pallas_call(
            pick_kernel,
            name="pick",
            out_shape=jax.ShapeDtypeStruct((outer, 4, per_req * BLK), f32),
            in_specs=[VMEM] * outer,
            out_specs=VMEM,
            compiler_params=small,
        )(*tgt_parts)
        tgt_parts.append(moved_inner(beside, "clus", 1))

    grad_src_pos, grad_src_weight, ids, live = pl.pallas_call(
        functools.partial(src_kernel, n_tgt, per_req),
        name="finish_src",
        out_shape=(
            jax.ShapeDtypeStruct((3, ns), f32),
            jax.ShapeDtypeStruct((1, ns), f32),
            jax.ShapeDtypeStruct((slots, 4, BLK), f32),
            jax.ShapeDtypeStruct((1, nt), f32),
        ),
        in_specs=[SMEM] * 3 + [VMEM] * (3 + n_tgt + outer),
        out_specs=(VMEM,) * 4,
        compiler_params=small,
    )(me, src_count, tgt_count, *src_side, *src_parts, *tgt_in)
    grad_tgt_pos, grad_tgt_weight = pl.pallas_call(
        functools.partial(tgt_kernel, outer, inner),
        name="finish_tgt",
        out_shape=(jax.ShapeDtypeStruct((3, nt), f32), jax.ShapeDtypeStruct((1, nt), f32)),
        in_specs=[VMEM] * (5 + len(tgt_parts)),
        out_specs=(VMEM,) * 2,
        compiler_params=small,
    )(*tgt_side, live, ids, *tgt_parts)
    return grad_src_pos, grad_src_weight.reshape(-1), grad_tgt_pos, grad_tgt_weight.reshape(-1)


def solution(mesh):
    placed = (
        P(None, ("clus", "tgt")),
        P(("clus", "tgt")),
        P(("clus", "tgt")),
        P(("clus", "tgt")),
        P(None, ("clus", "tgt")),
        P(("clus", "tgt")),
        P(("clus", "tgt")),
        P(("clus", "tgt")),
        P(("clus", "tgt"), None),
        P(("clus", "tgt")),
        P(("clus", "tgt")),
        P(("clus", "tgt")),
    )
    return jax.shard_map(
        shards,
        mesh=mesh,
        in_specs=placed,
        out_specs=(
            P(None, ("clus", "tgt")),
            P(("clus", "tgt")),
            P(None, ("clus", "tgt")),
            P(("clus", "tgt")),
        ),
        check_vma=False,
    )
```

```python
import functools
import math

import jax
import jax.numpy as jnp
from jax import lax
from jax.experimental import pallas as pl
from jax.experimental.pallas import tpu as pltpu
from jax.sharding import PartitionSpec as P

BLK = 256
LANES = 128
GROUP = 2
BUFS = 4

entropic = 0.05
LOG2E = math.log2(math.e)
SCALE = LOG2E / entropic
DEAD = -4096.0
PACK_VMEM = 60 * 2**20
MAIN_VMEM = 24 * 2**20

VMEM = pl.BlockSpec(memory_space=pltpu.VMEM)
SMEM = pl.BlockSpec(memory_space=pltpu.SMEM)
ANY = pl.BlockSpec(memory_space=pl.ANY)


def divide(x, n):
    shift = n.bit_length() - 1
    return lax.shift_right_logical(x, jnp.int32(shift)) if n == 1 << shift else lax.div(x, jnp.int32(n))


def step(i, k, n):
    return i ^ k if n & (n - 1) == 0 else (i + k) % n


def back(i, k, n):
    return i ^ k if n & (n - 1) == 0 else (i + n - k) % n


def flip(k, n):
    return k if n & (n - 1) == 0 else (n - k) % n


def split_axis(n):
    inner = 2 if n % 2 == 0 else 1
    return n // inner, inner


def moved(x, axis, k):
    n = lax.axis_size(axis)
    return lax.ppermute(x, axis, [(i, step(i, k, n)) for i in range(n)])


def moved_outer(x, axis, k):
    outer, inner = split_axis(lax.axis_size(axis))
    pairs = [(o * inner + i, step(o, k, outer) * inner + i) for o in range(outer) for i in range(inner)]
    return lax.ppermute(x, axis, pairs)


def moved_inner(x, axis, k):
    outer, inner = split_axis(lax.axis_size(axis))
    pairs = [(o * inner + i, o * inner + step(i, k, inner)) for o in range(outer) for i in range(inner)]
    return lax.ppermute(x, axis, pairs)


def live_row(count_ref, block):
    lane = lax.broadcasted_iota(jnp.int32, (1, BLK), 1)
    return lane < count_ref[block]


def pack_side(pos_ref, weight_ref, pot_ref, count_ref, out_ref):
    for b in range(count_ref.shape[0]):
        cols = slice(b * BLK, (b + 1) * BLK)
        pos = pos_ref[:, cols]
        norm = jnp.sum(pos * pos, axis=0, keepdims=True)
        expo = (pot_ref[:, cols] - 0.5 * norm) * SCALE + jnp.log(weight_ref[:, cols]) * LOG2E
        out_ref[0:3, cols] = pos
        out_ref[3:4, cols] = jnp.where(live_row(count_ref, b), expo, DEAD)


def pack_kernel(req_ref, sc_ref, tc_ref, ps_ref, pq_ref, sp_ref, sw_ref, so_ref, tp_ref, tw_ref, to_ref, src_ref, tgt_ref):
    pack_side(sp_ref, sw_ref, so_ref, sc_ref, src_ref)
    pack_side(tp_ref, tw_ref, to_ref, tc_ref, tgt_ref)
    per, rows = req_ref.shape
    own = tp_ref.shape[1]
    lane = lax.broadcasted_iota(jnp.int32, (1, tgt_ref.shape[1] - own), 1)
    ids = jnp.zeros(lane.shape, jnp.float32)
    for r in range(rows):
        for m in range(per):
            ids = jnp.where(lane == r * per + m, req_ref[m, r].astype(jnp.float32), ids)
    tgt_ref[:, own:] = jnp.zeros((4,) + lane.shape[1:], jnp.float32)
    tgt_ref[0:1, own:] = ids
    tgt_ref[1:2, own : own + ps_ref.shape[1]] = ps_ref[...].astype(jnp.float32)
    tgt_ref[2:3, own : own + pq_ref.shape[1]] = pq_ref[...].astype(jnp.float32)


def split3(x):
    high = x.astype(jnp.bfloat16).astype(jnp.float32)
    rest = x - high
    mid = rest.astype(jnp.bfloat16).astype(jnp.float32)
    return high, mid, rest - mid


def stages(outer):
    cuts = [(0, 1), (outer - 1, outer), (1, outer - 1)]
    return [(first, stop) for i, (first, stop) in enumerate(cuts) if first < stop and (i == 0 or first > 0)]


def dot(x, y):
    return jnp.dot(x, y, preferred_element_type=jnp.float32)


def dot_t(x, y):
    return lax.dot_general(x, y, (((1,), (1,)), ((), ())), preferred_element_type=jnp.float32)


def away(i, me, n):
    return i ^ me if n & (n - 1) == 0 else lax.rem(me - i + n, n)


def is_power(n):
    return n & (n - 1) == 0


def local_block(s, me, n, per_dev):
    if is_power(n) and is_power(per_dev):
        return s ^ (me * per_dev)
    dev = divide(s, per_dev)
    return s + (away(dev, me, n) - dev) * per_dev


def local_slot(q, outer_me, inner_me, outer, inner, per_req):
    if is_power(outer) and is_power(inner) and is_power(per_req):
        return q ^ ((outer_me * inner + inner_me) * per_req)
    clus = divide(q, per_req)
    place = divide(clus, inner)
    side = away(clus - place * inner, inner_me, inner)
    return (away(place, outer_me, outer) * inner + side - clus) * per_req + q


def prepare_src(src_in, left, src_rows):
    last = lax.broadcasted_iota(jnp.int32, (4, BLK), 0) == 3
    pad = jnp.zeros((8, BLK), jnp.float32)
    per_dev = src_in[0].shape[1] // BLK
    for k, part in enumerate(src_in):
        for b in range(per_dev):
            high, mid, low = split3(part[:, b * BLK : (b + 1) * BLK])
            high1, mid1 = jnp.where(last, 1.0, high), jnp.where(last, 1.0, mid)
            place = k * per_dev + b
            left[place] = jnp.concatenate([high, high1, high1, mid, mid1, low, pad], 0).astype(jnp.bfloat16)
            src_rows[place] = jnp.concatenate([high1, jnp.where(last, 0.0, mid)], 0)
    dead = lax.broadcasted_iota(jnp.int32, (32, BLK), 0) == 3
    left[len(src_in) * per_dev] = jnp.where(dead, DEAD, 0.0).astype(jnp.bfloat16)
    src_rows[len(src_in) * per_dev] = pad


def prepare_tgt(slot, block, rows, tgt_in, right, tgt_rows):
    last = lax.broadcasted_iota(jnp.int32, (4, BLK), 0) == 3
    pad = jnp.zeros((8, BLK), jnp.float32)
    raw = tgt_in[rows, pl.ds(pl.multiple_of(block * BLK, BLK), BLK)]
    high, mid, _ = split3(raw)
    tgt_rows[slot] = jnp.concatenate([jnp.where(last, 1.0, high), jnp.where(last, 0.0, mid)], 0)
    high, mid, low = split3(jnp.where(last, raw, raw * SCALE))
    high1 = jnp.where(last, 1.0, high)
    wide = jnp.concatenate([high1, mid, low, high1, jnp.where(last, high, mid), high1, pad], 0)
    right[slot] = wide.T.astype(jnp.bfloat16)


def pairs_kernel(n_tgt, n_clus, per_req, turn, *refs):
    outer, inner = split_axis(n_clus)
    cuts = stages(outer)
    first, stop = cuts[turn]
    begins, ends = turn == 0, turn == len(cuts) - 1
    slots = n_clus * per_req
    refs = list(refs)
    take = lambda n: [refs.pop(0) for _ in range(n)]
    if begins:
        (far_me,) = take(1)
        src_in = take(n_tgt)
    else:
        memo, left, src_rows, src_sums = take(4)
    tgt_in = take(stop - first)
    held = [k for cut in cuts[1:turn] for k in range(*cut)] if ends else []
    held_in = take(len(held))
    if begins and not ends:
        memo, left, src_rows = take(3)
    src_out = take(n_tgt if ends else 1)
    tgt_out = take(stop - first)
    for far, near in zip(held_in, take(len(held))):
        near[...] = far[...]
    src_acc = take(1)[0] if ends else src_out[0]
    if begins and ends:
        memo, left, src_rows = take(3)
    right, tgt_rows, tgt_acc, *refs = refs
    if begins:
        (chosen_src, chosen_slot, sem, me_ref, head), kern_bufs = refs[:5], refs[5:]
        copy = pltpu.make_async_copy(far_me, me_ref, sem)
        copy.start()
        head[...] = tgt_in[0][0:4, tgt_in[0].shape[1] - head.shape[1] :].astype(jnp.int32)
    else:
        kern_bufs = refs
    n_src = left.shape[0] - 1
    per_dev = n_src // n_tgt
    if begins:
        prepare_src(src_in, left, src_rows)
        src_acc[...] = jnp.zeros_like(src_acc)
    else:
        src_acc[...] = src_sums[...]
    tgt_acc[...] = jnp.zeros_like(tgt_acc)

    pairs = (memo.shape[0] - len(cuts) - slots) // (2 * len(cuts))
    tops = [len(cuts) + slots + 2 * pairs * i for i in range(len(cuts))]

    def note(row, value):
        memo[pl.ds(row, 1), :] = jnp.full((1, LANES), value, jnp.int32)

    if begins:
        copy.wait()
        tgt_me, outer_me, inner_me, count = (me_ref[i] for i in range(4))
        for slot in range(slots):
            note(len(cuts) + local_slot(slot, outer_me, inner_me, outer, inner, per_req), head[0, slot])
        totals = [jnp.int32(0)] * len(cuts)
        for pair in range(pairs):
            s = local_block(head[1, pair], tgt_me, n_tgt, per_dev)
            slot = local_slot(head[2, pair], outer_me, inner_me, outer, inner, per_req)
            for i, (low, high) in enumerate(cuts):
                inside = slot - low * inner * per_req
                if i == 0:
                    chosen_src[totals[0]] = s
                    chosen_slot[totals[0]] = inside
                else:
                    note(tops[i] + totals[i], s)
                    note(tops[i] + pairs + totals[i], inside)
                hit = (pair < count) & (inside >= 0) & (inside < (high - low) * inner * per_req)
                totals[i] = totals[i] + hit.astype(jnp.int32)
        for i in range(1, len(cuts)):
            note(i, totals[i])
        total = totals[0]
    else:
        total = memo[turn, 0]
    for slot in range((stop - first) * inner * per_req):
        i = slot // per_req % inner
        block = memo[len(cuts) + first * inner * per_req + slot, 0]
        prepare_tgt(slot, block, slice(4 * i, 4 * i + 4), tgt_in[slot // (inner * per_req)], right, tgt_rows)

    def pair_ids(entry):
        inside = jnp.minimum(entry, pairs - 1)
        live = entry < total
        if begins:
            s, q = chosen_src[inside], chosen_slot[inside]
        else:
            s, q = memo[tops[turn] + inside, 0], memo[tops[turn] + pairs + inside, 0]
        return jnp.where(live, s, n_src), jnp.where(live, q, 0)

    def weigh(entry, buf, g):
        s, q = pair_ids(entry)
        kern = jnp.exp2(dot(right[q], left[s]))
        high = kern.astype(jnp.bfloat16)
        buf[g, 0] = high
        buf[g, 1] = (kern - high.astype(jnp.float32)).astype(jnp.bfloat16)

    def reduce(entry, buf, g):
        s, q = pair_ids(entry)
        high, low = buf[g, 0], buf[g, 1]
        y = tgt_rows[q].astype(jnp.bfloat16)
        x = src_rows[s].astype(jnp.bfloat16)
        return s, q, dot(y, high) + dot(y, low), dot_t(x, high) + dot_t(x, low)

    bufs = len(kern_bufs)
    for g in range(GROUP):
        weigh(g, kern_bufs[0], g)

    def body(trip, carry):
        start = trip * bufs * GROUP
        for u in range(bufs):
            parts = []
            for g in range(GROUP):
                weigh(start + (u + 1) * GROUP + g, kern_bufs[(u + 1) % bufs], g)
                parts.append(reduce(start + u * GROUP + g, kern_bufs[u], g))
            for s, q, src_part, tgt_part in parts:
                src_acc[s] += src_part
                tgt_acc[q] += tgt_part
        return carry

    lax.fori_loop(0, divide(total + GROUP * bufs - 1, GROUP * bufs), body, 0)

    for place in range((stop - first) * inner):
        for m in range(per_req):
            part = tgt_acc[place * per_req + m]
            tgt_out[place // inner][place % inner, :, m * BLK : (m + 1) * BLK] = part[0:4] + part[4:8]
    if ends:
        for k in range(n_tgt):
            base = flip(k, n_tgt) * per_dev
            for b in range(per_dev):
                part = src_acc[base + b]
                src_out[k][:, b * BLK : (b + 1) * BLK] = part[0:4] + part[4:8]


def join_kernel(*refs):
    *parts, out_ref = refs
    for k, part in enumerate(parts):
        out_ref[4 * k : 4 * k + 4] = part[...]


def keep_kernel(*refs):
    refs[-1][...] = refs[0][...]


def pick_kernel(*refs):
    *parts, out_ref = refs
    for k, part in enumerate(parts):
        out_ref[k] = part[1]


def finish_side(pos, weight, pot, live, total):
    mass = total[3:4]
    return pos * mass - total[0:3], jnp.where(live, pot - entropic * mass / weight, 0.0)


def src_kernel(n_tgt, per_req, me_ref, src_count_ref, tgt_count_ref, pos_ref, weight_ref, pot_ref, *refs):
    parts, refs = refs[:n_tgt], refs[n_tgt:]
    *tgt_in, grad_pos_ref, grad_weight_ref, ids_ref, live_ref = refs
    for b in range(src_count_ref.shape[0]):
        cols = slice(b * BLK, (b + 1) * BLK)
        grad_pos_ref[:, cols], grad_weight_ref[:, cols] = finish_side(
            pos_ref[:, cols],
            weight_ref[:, cols],
            pot_ref[:, cols],
            live_row(src_count_ref, b),
            sum(p[:, cols] for p in parts),
        )
    for b in range(tgt_count_ref.shape[0]):
        live_ref[:, b * BLK : (b + 1) * BLK] = live_row(tgt_count_ref, b).astype(jnp.float32)
    outer = len(tgt_in)
    inner = tgt_in[0].shape[0] // 4
    outer_me, inner_me = me_ref[1], me_ref[2]
    me = outer_me * inner + inner_me
    own = tgt_count_ref.shape[0] * BLK
    width = tgt_in[0].shape[1] - own
    lane = lax.broadcasted_iota(jnp.int32, (1, width), 1)
    for k in range(outer):
        for i in range(inner):
            row = tgt_in[flip(k, outer)][4 * i : 4 * i + 1, own:]
            for m in range(per_req):
                block = jnp.sum(jnp.where(lane == me * per_req + m, row, 0.0), axis=1, keepdims=True)
                ids_ref[(k * inner + i) * per_req + m] = jnp.broadcast_to(block, (4, BLK))


def tgt_kernel(outer, inner, pos_ref, weight_ref, pot_ref, live_ref, ids_ref, *refs):
    *parts, grad_pos_ref, grad_weight_ref = refs
    own, side = parts[:outer], parts[outer:]
    per_req = ids_ref.shape[0] // (outer * inner)
    for b in range(pos_ref.shape[1] // BLK):
        cols = slice(b * BLK, (b + 1) * BLK)
        total = jnp.zeros((4, BLK), jnp.float32)
        for k in range(outer):
            for i in range(inner):
                for m in range(per_req):
                    wide = slice(m * BLK, (m + 1) * BLK)
                    part = own[k][0, :, wide] if i == 0 else side[i - 1][k, :, wide]
                    total += jnp.where(ids_ref[(k * inner + i) * per_req + m] == b, part, 0.0)
        grad_pos_ref[:, cols], grad_weight_ref[:, cols] = finish_side(
            pos_ref[:, cols], weight_ref[:, cols], pot_ref[:, cols], live_ref[:, cols] > 0.0, total
        )


def shards(
    src_pos,
    src_weight,
    src_pot,
    src_count,
    tgt_pos,
    tgt_weight,
    tgt_pot,
    tgt_count,
    requests,
    pair_src,
    pair_slot,
    pair_count,
):
    f32 = jnp.float32
    n_tgt, n_clus = lax.axis_size("tgt"), lax.axis_size("clus")
    outer, inner = split_axis(n_clus)
    ns, nt = src_pos.shape[1], tgt_pos.shape[1]
    n_src = n_tgt * (ns // BLK)
    per_req = requests.shape[1]
    slots = n_clus * per_req
    width = -(-max(slots, pair_src.shape[0]) // LANES) * LANES
    asked = requests.T
    small = pltpu.CompilerParams(vmem_limit_bytes=MAIN_VMEM)
    clus_me = lax.axis_index("clus")
    me = jnp.stack([lax.axis_index("tgt"), clus_me // inner, clus_me % inner, pair_count[0]]).astype(jnp.int32)
    src_side = (src_pos, src_weight.reshape(1, -1), src_pot.reshape(1, -1))
    tgt_side = (tgt_pos, tgt_weight.reshape(1, -1), tgt_pot.reshape(1, -1))

    src_pack, tgt_pack = pl.pallas_call(
        pack_kernel,
        name="pack",
        out_shape=(jax.ShapeDtypeStruct((4, ns), f32), jax.ShapeDtypeStruct((4, nt + width), f32)),
        in_specs=[SMEM] * 3 + [VMEM] * 8,
        out_specs=(VMEM, VMEM),
        compiler_params=pltpu.CompilerParams(vmem_limit_bytes=PACK_VMEM),
    )(asked, src_count, tgt_count, pair_src.reshape(1, -1), pair_slot.reshape(1, -1), *src_side, *tgt_side)

    src_in = [src_pack] + [moved(src_pack, "tgt", k) for k in range(1, n_tgt)]
    near = [tgt_pack] + [moved_inner(tgt_pack, "clus", k) for k in range(1, inner)]
    near = pl.pallas_call(
        join_kernel,
        name="join",
        out_shape=jax.ShapeDtypeStruct((4 * inner, nt + width), f32),
        in_specs=[VMEM] * inner,
        out_specs=VMEM,
        compiler_params=small,
    )(*near)
    tgt_in = [near] + [moved_outer(near, "clus", k) for k in range(1, outer)]

    block_rows = jax.ShapeDtypeStruct((n_src + 1, 8, BLK), f32)
    left_side = jax.ShapeDtypeStruct((n_src + 1, 32, BLK), jnp.bfloat16)
    n_pairs = pair_src.shape[0]
    memo_rows = jax.ShapeDtypeStruct((len(stages(outer)) * (1 + 2 * n_pairs) + slots, LANES), jnp.int32)
    list_scratch = (
        [pltpu.SMEM((n_pairs + 1,), jnp.int32)] * 2
        + [pltpu.SemaphoreType.DMA, pltpu.SMEM(me.shape, jnp.int32)]
        + [pltpu.VMEM((4, width), jnp.int32)]
    )
    kern_bufs = [pltpu.VMEM((GROUP, 2, BLK, BLK), jnp.bfloat16)] * BUFS
    part_shape = jax.ShapeDtypeStruct((inner, 4, per_req * BLK), f32)
    state, sums = (), {}
    for turn, (first, stop) in enumerate(stages(outer)):
        begins, ends = turn == 0, turn == len(stages(outer)) - 1
        held = [k for cut in stages(outer)[1:turn] for k in range(*cut)] if ends else []
        args = ([me] + src_in if begins else list(state)) + tgt_in[first:stop] + [sums[k] for k in held]
        outs = [memo_rows, left_side, block_rows] if begins and not ends else []
        outs += [jax.ShapeDtypeStruct((4, ns), f32)] * n_tgt if ends else [block_rows]
        outs += [part_shape] * (stop - first + len(held))
        extra = [pltpu.VMEM(block_rows.shape, f32)] if ends else []
        if begins and ends:
            extra += [pltpu.VMEM(memo_rows.shape, jnp.int32)]
            extra += [pltpu.VMEM(left_side.shape, jnp.bfloat16), pltpu.VMEM(block_rows.shape, f32)]
        near = (stop - first) * inner * per_req
        extra += [
            pltpu.VMEM((near, BLK, 32), jnp.bfloat16),
            pltpu.VMEM((near, 8, BLK), f32),
            pltpu.VMEM((near, 8, BLK), f32),
        ]
        res = pl.pallas_call(
            functools.partial(pairs_kernel, n_tgt, n_clus, per_req, turn),
            name=f"pairs_{first}_{stop}",
            out_shape=outs,
            in_specs=[ANY if begins and a is me else VMEM for a in args],
            out_specs=[VMEM] * len(outs),
            scratch_shapes=extra + (list_scratch if begins else []) + kern_bufs,
            compiler_params=small,
            cost_estimate=pl.CostEstimate(flops=4*10**8 if begins else 0, bytes_accessed=2**20, transcendentals=0),
        )(*args)
        made = list(range(first, stop)) + held
        sums.update(zip(made, res[len(res) - len(made) :]))
        if ends:
            src_out = res[:n_tgt]
        else:
            state = tuple(res[:4]) if begins else state[:3] + (res[0],)

    src_parts = [src_out[0]] + [moved(src_out[k], "tgt", k) for k in range(1, n_tgt)]
    tgt_parts = [sums[0]] + [moved_outer(sums[k], "clus", flip(k, outer)) for k in range(1, outer)]
    part_keep = functools.partial(
        pl.pallas_call,
        keep_kernel,
        name="keep",
        out_shape=part_shape,
        out_specs=VMEM,
        compiler_params=small,
    )
    for k in reversed(range(2, outer)):
        late = tgt_parts[k + 1 : k + 2]
        tgt_parts[k] = part_keep(in_specs=[VMEM] * (1 + len(late)))(tgt_parts[k], *late)
    if inner == 2:
        beside = pl.pallas_call(
            pick_kernel,
            name="pick",
            out_shape=jax.ShapeDtypeStruct((outer, 4, per_req * BLK), f32),
            in_specs=[VMEM] * outer,
            out_specs=VMEM,
            compiler_params=small,
        )(*tgt_parts)
        tgt_parts.append(moved_inner(beside, "clus", 1))

    grad_src_pos, grad_src_weight, ids, live = pl.pallas_call(
        functools.partial(src_kernel, n_tgt, per_req),
        name="finish_src",
        out_shape=(
            jax.ShapeDtypeStruct((3, ns), f32),
            jax.ShapeDtypeStruct((1, ns), f32),
            jax.ShapeDtypeStruct((slots, 4, BLK), f32),
            jax.ShapeDtypeStruct((1, nt), f32),
        ),
        in_specs=[SMEM] * 3 + [VMEM] * (3 + n_tgt + outer),
        out_specs=(VMEM,) * 4,
        compiler_params=small,
    )(me, src_count, tgt_count, *src_side, *src_parts, *tgt_in)
    grad_tgt_pos, grad_tgt_weight = pl.pallas_call(
        functools.partial(tgt_kernel, outer, inner),
        name="finish_tgt",
        out_shape=(jax.ShapeDtypeStruct((3, nt), f32), jax.ShapeDtypeStruct((1, nt), f32)),
        in_specs=[VMEM] * (5 + len(tgt_parts)),
        out_specs=(VMEM,) * 2,
        compiler_params=small,
    )(*tgt_side, live, ids, *tgt_parts)
    return grad_src_pos, grad_src_weight.reshape(-1), grad_tgt_pos, grad_tgt_weight.reshape(-1)


def solution(mesh):
    placed = (
        P(None, ("clus", "tgt")),
        P(("clus", "tgt")),
        P(("clus", "tgt")),
        P(("clus", "tgt")),
        P(None, ("clus", "tgt")),
        P(("clus", "tgt")),
        P(("clus", "tgt")),
        P(("clus", "tgt")),
        P(("clus", "tgt"), None),
        P(("clus", "tgt")),
        P(("clus", "tgt")),
        P(("clus", "tgt")),
    )
    return jax.shard_map(
        shards,
        mesh=mesh,
        in_specs=placed,
        out_specs=(
            P(None, ("clus", "tgt")),
            P(("clus", "tgt")),
            P(None, ("clus", "tgt")),
            P(("clus", "tgt")),
        ),
        check_vma=False,
    )
```

```python
import functools
import math

import jax
import jax.numpy as jnp
from jax import lax
from jax.experimental import pallas as pl
from jax.experimental.pallas import tpu as pltpu
from jax.sharding import PartitionSpec as P

BLK = 256
LANES = 128
GROUP = 2
BUFS = 4
MIX = 2**10

entropic = 0.05
LOG2E = math.log2(math.e)
SCALE = LOG2E / entropic
DEAD = -4096.0
PACK_VMEM = 60 * 2**20
MAIN_VMEM = 24 * 2**20

VMEM = pl.BlockSpec(memory_space=pltpu.VMEM)
SMEM = pl.BlockSpec(memory_space=pltpu.SMEM)
ANY = pl.BlockSpec(memory_space=pl.ANY)


def divide(x, n):
    shift = n.bit_length() - 1
    return lax.shift_right_logical(x, jnp.int32(shift)) if n == 1 << shift else lax.div(x, jnp.int32(n))


def step(i, k, n):
    return i ^ k if n & (n - 1) == 0 else (i + k) % n


def back(i, k, n):
    return i ^ k if n & (n - 1) == 0 else (i + n - k) % n


def flip(k, n):
    return k if n & (n - 1) == 0 else (n - k) % n


def split_axis(n):
    inner = 2 if n % 2 == 0 else 1
    return n // inner, inner


def moved(x, axis, k):
    n = lax.axis_size(axis)
    return lax.ppermute(x, axis, [(i, step(i, k, n)) for i in range(n)])


def moved_outer(x, axis, k):
    outer, inner = split_axis(lax.axis_size(axis))
    pairs = [(o * inner + i, step(o, k, outer) * inner + i) for o in range(outer) for i in range(inner)]
    return lax.ppermute(x, axis, pairs)


def moved_inner(x, axis, k):
    outer, inner = split_axis(lax.axis_size(axis))
    pairs = [(o * inner + i, o * inner + step(i, k, inner)) for o in range(outer) for i in range(inner)]
    return lax.ppermute(x, axis, pairs)


def live_row(count_ref, block):
    lane = lax.broadcasted_iota(jnp.int32, (1, BLK), 1)
    return lane < count_ref[block]


def pack_side(pos_ref, weight_ref, pot_ref, count_ref, out_ref):
    for b in range(count_ref.shape[0]):
        cols = slice(b * BLK, (b + 1) * BLK)
        pos = pos_ref[:, cols]
        norm = jnp.sum(pos * pos, axis=0, keepdims=True)
        expo = (pot_ref[:, cols] - 0.5 * norm) * SCALE + jnp.log(weight_ref[:, cols]) * LOG2E
        out_ref[0:3, cols] = pos
        out_ref[3:4, cols] = jnp.where(live_row(count_ref, b), expo, DEAD)


def pack_kernel(req_ref, sc_ref, tc_ref, ps_ref, pq_ref, sp_ref, sw_ref, so_ref, tp_ref, tw_ref, to_ref, src_ref, tgt_ref):
    pack_side(sp_ref, sw_ref, so_ref, sc_ref, src_ref)
    pack_side(tp_ref, tw_ref, to_ref, tc_ref, tgt_ref)
    per, rows = req_ref.shape
    own = tp_ref.shape[1]
    lane = lax.broadcasted_iota(jnp.int32, (1, tgt_ref.shape[1] - own), 1)
    ids = jnp.zeros(lane.shape, jnp.float32)
    for r in range(rows):
        for m in range(per):
            ids = jnp.where(lane == r * per + m, req_ref[m, r].astype(jnp.float32), ids)
    tgt_ref[:, own:] = jnp.zeros((4,) + lane.shape[1:], jnp.float32)
    tgt_ref[0:1, own:] = ids
    tgt_ref[1:2, own : own + ps_ref.shape[1]] = (ps_ref[...] * MIX + pq_ref[...]).astype(jnp.float32)


def split3(x):
    high = x.astype(jnp.bfloat16).astype(jnp.float32)
    rest = x - high
    mid = rest.astype(jnp.bfloat16).astype(jnp.float32)
    return high, mid, rest - mid


def stages(outer):
    halves = [outer - 1] if outer > 2 else []
    rest = [k for k in reversed(range(1, outer)) if k not in halves]
    return [cut for cut in ([0], halves, rest) if cut]


def dot(x, y):
    return jnp.dot(x, y, preferred_element_type=jnp.float32)


def dot_t(x, y):
    return lax.dot_general(x, y, (((1,), (1,)), ((), ())), preferred_element_type=jnp.float32)


def away(i, me, n):
    return i ^ me if n & (n - 1) == 0 else lax.rem(me - i + n, n)


def is_power(n):
    return n & (n - 1) == 0


def local_block(s, me, n, per_dev):
    if is_power(n) and is_power(per_dev):
        return s ^ (me * per_dev)
    dev = divide(s, per_dev)
    return s + (away(dev, me, n) - dev) * per_dev


def local_slot(q, outer_me, inner_me, outer, inner, per_req):
    if is_power(outer) and is_power(inner) and is_power(per_req):
        return q ^ ((outer_me * inner + inner_me) * per_req)
    clus = divide(q, per_req)
    place = divide(clus, inner)
    side = away(clus - place * inner, inner_me, inner)
    return (away(place, outer_me, outer) * inner + side - clus) * per_req + q


def prepare_src(src_in, left, src_rows):
    last = lax.broadcasted_iota(jnp.int32, (4, BLK), 0) == 3
    pad = jnp.zeros((8, BLK), jnp.float32)
    per_dev = src_in[0].shape[1] // BLK
    for k, part in enumerate(src_in):
        for b in range(per_dev):
            high, mid, low = split3(part[:, b * BLK : (b + 1) * BLK])
            high1, mid1 = jnp.where(last, 1.0, high), jnp.where(last, 1.0, mid)
            place = k * per_dev + b
            left[place] = jnp.concatenate([high, high1, high1, mid, mid1, low, pad], 0).astype(jnp.bfloat16)
            src_rows[place] = jnp.concatenate([high1, jnp.where(last, 0.0, mid)], 0)
    dead = lax.broadcasted_iota(jnp.int32, (32, BLK), 0) == 3
    left[len(src_in) * per_dev] = jnp.where(dead, DEAD, 0.0).astype(jnp.bfloat16)
    src_rows[len(src_in) * per_dev] = pad


def prepare_tgt(slot, block, rows, tgt_in, right, tgt_rows):
    last = lax.broadcasted_iota(jnp.int32, (4, BLK), 0) == 3
    pad = jnp.zeros((8, BLK), jnp.float32)
    raw = tgt_in[rows, pl.ds(pl.multiple_of(block * BLK, BLK), BLK)]
    high, mid, _ = split3(raw)
    tgt_rows[slot] = jnp.concatenate([jnp.where(last, 1.0, high), jnp.where(last, 0.0, mid)], 0)
    high, mid, low = split3(jnp.where(last, raw, raw * SCALE))
    high1 = jnp.where(last, 1.0, high)
    wide = jnp.concatenate([high1, mid, low, high1, jnp.where(last, high, mid), high1, pad], 0)
    right[slot] = wide.T.astype(jnp.bfloat16)


def pairs_kernel(n_tgt, n_clus, per_req, turn, *refs):
    outer, inner = split_axis(n_clus)
    cuts = stages(outer)
    mine = cuts[turn]
    wide = inner * per_req
    begins, ends = turn == 0, turn == len(cuts) - 1
    slots = n_clus * per_req
    refs = list(refs)
    take = lambda n: [refs.pop(0) for _ in range(n)]
    if begins:
        count_ref, _ = take(2)
        src_in = take(n_tgt)
    else:
        memo, left, src_rows, src_sums = take(4)
    tgt_in = take(len(mine))
    held = [k for cut in cuts[1:turn] for k in cut] if ends else []
    held_in = take(len(held))
    if begins and not ends:
        memo, left, src_rows = take(3)
    src_out = take(n_tgt if ends else 1)
    tgt_out = take(len(mine))
    for far, near in zip(held_in, take(len(held))):
        near[...] = far[...]
    src_acc = take(1)[0] if ends else src_out[0]
    if begins and ends:
        memo, left, src_rows = take(3)
    right, tgt_rows, tgt_acc, *refs = refs
    if begins:
        (chosen_src, chosen_slot, head), kern_bufs = refs[:3], refs[3:]
        head[...] = tgt_in[0][0:4, tgt_in[0].shape[1] - head.shape[1] :].astype(jnp.int32)
    else:
        kern_bufs = refs
    n_src = left.shape[0] - 1
    per_dev = n_src // n_tgt
    if begins:
        prepare_src(src_in, left, src_rows)
        src_acc[...] = jnp.zeros_like(src_acc)
    else:
        src_acc[...] = src_sums[...]
    tgt_acc[...] = jnp.zeros_like(tgt_acc)

    pairs = (memo.shape[0] - len(cuts) - slots) // len(cuts)
    tops = [len(cuts) + slots + pairs * i for i in range(len(cuts))]

    def note(row, value):
        memo[pl.ds(row, 1), :] = jnp.full((1, LANES), value, jnp.int32)

    if begins:
        count, tgt_me, clus_me = count_ref[0], lax.axis_index("tgt"), lax.axis_index("clus")
        outer_me = divide(clus_me, inner)
        inner_me = clus_me - outer_me * inner
        for slot in range(slots):
            note(len(cuts) + local_slot(slot, outer_me, inner_me, outer, inner, per_req), head[0, slot])
        totals = [jnp.int32(0)] * len(cuts)
        for pair in range(pairs):
            both = head[1, pair]
            s = local_block(divide(both, MIX), tgt_me, n_tgt, per_dev)
            slot = local_slot(both & (MIX - 1), outer_me, inner_me, outer, inner, per_req)
            k = divide(slot, wide)
            for i, cut in enumerate(cuts):
                if i == 0:
                    chosen_src[totals[0]] = s
                    chosen_slot[totals[0]] = slot
                else:
                    note(tops[i] + totals[i], s * MIX + slot)
                held_here = sum((k == far).astype(jnp.int32) for far in cut)
                totals[i] = totals[i] + jnp.where(pair < count, held_here, 0)
        for i in range(1, len(cuts)):
            note(i, totals[i])
        total = totals[0]
    else:
        total = memo[turn, 0]
    for place, k in enumerate(mine):
        for i in range(inner):
            for m in range(per_req):
                slot = k * wide + i * per_req + m
                block = memo[len(cuts) + slot, 0]
                prepare_tgt(slot, block, slice(4 * i, 4 * i + 4), tgt_in[place], right, tgt_rows)

    def pair_ids(entry):
        inside = jnp.minimum(entry, pairs - 1)
        live = entry < total
        if begins:
            s, q = chosen_src[inside], chosen_slot[inside]
        else:
            both = memo[tops[turn] + inside, 0]
            s, q = divide(both, MIX), both & (MIX - 1)
        return jnp.where(live, s, n_src), jnp.where(live, q, mine[0] * wide)

    def weigh(entry, buf, g):
        s, q = pair_ids(entry)
        kern = jnp.exp2(dot(right[q], left[s]))
        high = kern.astype(jnp.bfloat16)
        buf[g, 0] = high
        buf[g, 1] = (kern - high.astype(jnp.float32)).astype(jnp.bfloat16)

    def reduce(entry, buf, g):
        s, q = pair_ids(entry)
        high, low = buf[g, 0], buf[g, 1]
        y = tgt_rows[q].astype(jnp.bfloat16)
        x = src_rows[s].astype(jnp.bfloat16)
        return s, q, dot(y, high) + dot(y, low), dot_t(x, high) + dot_t(x, low)

    bufs = len(kern_bufs)
    for g in range(GROUP):
        weigh(g, kern_bufs[0], g)

    def body(trip, carry):
        start = trip * bufs * GROUP
        for u in range(bufs):
            parts = []
            for g in range(GROUP):
                weigh(start + (u + 1) * GROUP + g, kern_bufs[(u + 1) % bufs], g)
                parts.append(reduce(start + u * GROUP + g, kern_bufs[u], g))
            for s, q, src_part, tgt_part in parts:
                src_acc[s] += src_part
                tgt_acc[q] += tgt_part
        return carry

    lax.fori_loop(0, divide(total + GROUP * bufs - 1, GROUP * bufs), body, 0)

    for place, k in enumerate(mine):
        for i in range(inner):
            for m in range(per_req):
                part = tgt_acc[k * wide + i * per_req + m]
                tgt_out[place][i, :, m * BLK : (m + 1) * BLK] = part[0:4] + part[4:8]
    if ends:
        for k in range(n_tgt):
            base = flip(k, n_tgt) * per_dev
            for b in range(per_dev):
                part = src_acc[base + b]
                src_out[k][:, b * BLK : (b + 1) * BLK] = part[0:4] + part[4:8]


def join_kernel(*refs):
    *parts, out_ref = refs
    for k, part in enumerate(parts):
        out_ref[4 * k : 4 * k + 4] = part[...]


def keep_kernel(*refs):
    refs[-1][...] = refs[0][...]


def pick_kernel(*refs):
    *parts, out_ref = refs
    for k, part in enumerate(parts):
        out_ref[k] = part[1]


def finish_side(pos, weight, pot, live, total):
    mass = total[3:4]
    return pos * mass - total[0:3], jnp.where(live, pot - entropic * mass / weight, 0.0)


def src_kernel(n_tgt, per_req, me_ref, src_count_ref, tgt_count_ref, pos_ref, weight_ref, pot_ref, *refs):
    parts, refs = refs[:n_tgt], refs[n_tgt:]
    *tgt_in, grad_pos_ref, grad_weight_ref, ids_ref, live_ref = refs
    for b in range(src_count_ref.shape[0]):
        cols = slice(b * BLK, (b + 1) * BLK)
        grad_pos_ref[:, cols], grad_weight_ref[:, cols] = finish_side(
            pos_ref[:, cols],
            weight_ref[:, cols],
            pot_ref[:, cols],
            live_row(src_count_ref, b),
            sum(p[:, cols] for p in parts),
        )
    for b in range(tgt_count_ref.shape[0]):
        live_ref[:, b * BLK : (b + 1) * BLK] = live_row(tgt_count_ref, b).astype(jnp.float32)
    outer = len(tgt_in)
    inner = tgt_in[0].shape[0] // 4
    outer_me, inner_me = me_ref[1], me_ref[2]
    me = outer_me * inner + inner_me
    own = tgt_count_ref.shape[0] * BLK
    width = tgt_in[0].shape[1] - own
    lane = lax.broadcasted_iota(jnp.int32, (1, width), 1)
    for k in range(outer):
        for i in range(inner):
            row = tgt_in[flip(k, outer)][4 * i : 4 * i + 1, own:]
            for m in range(per_req):
                block = jnp.sum(jnp.where(lane == me * per_req + m, row, 0.0), axis=1, keepdims=True)
                ids_ref[(k * inner + i) * per_req + m] = jnp.broadcast_to(block, (4, BLK))


def tgt_kernel(outer, inner, pos_ref, weight_ref, pot_ref, live_ref, ids_ref, *refs):
    *parts, grad_pos_ref, grad_weight_ref = refs
    own, side = parts[:outer], parts[outer:]
    per_req = ids_ref.shape[0] // (outer * inner)
    for b in range(pos_ref.shape[1] // BLK):
        cols = slice(b * BLK, (b + 1) * BLK)
        total = jnp.zeros((4, BLK), jnp.float32)
        for k in range(outer):
            for i in range(inner):
                for m in range(per_req):
                    wide = slice(m * BLK, (m + 1) * BLK)
                    part = own[k][0, :, wide] if i == 0 else side[i - 1][k, :, wide]
                    total += jnp.where(ids_ref[(k * inner + i) * per_req + m] == b, part, 0.0)
        grad_pos_ref[:, cols], grad_weight_ref[:, cols] = finish_side(
            pos_ref[:, cols], weight_ref[:, cols], pot_ref[:, cols], live_ref[:, cols] > 0.0, total
        )


def shards(
    src_pos,
    src_weight,
    src_pot,
    src_count,
    tgt_pos,
    tgt_weight,
    tgt_pot,
    tgt_count,
    requests,
    pair_src,
    pair_slot,
    pair_count,
):
    f32 = jnp.float32
    n_tgt, n_clus = lax.axis_size("tgt"), lax.axis_size("clus")
    outer, inner = split_axis(n_clus)
    ns, nt = src_pos.shape[1], tgt_pos.shape[1]
    n_src = n_tgt * (ns // BLK)
    per_req = requests.shape[1]
    slots = n_clus * per_req
    width = -(-max(slots, pair_src.shape[0]) // LANES) * LANES
    asked = requests.T
    small = pltpu.CompilerParams(vmem_limit_bytes=MAIN_VMEM)
    clus_me = lax.axis_index("clus")
    me = jnp.stack([lax.axis_index("tgt"), clus_me // inner, clus_me % inner, pair_count[0]]).astype(jnp.int32)
    src_side = (src_pos, src_weight.reshape(1, -1), src_pot.reshape(1, -1))
    tgt_side = (tgt_pos, tgt_weight.reshape(1, -1), tgt_pot.reshape(1, -1))

    src_pack, tgt_pack = pl.pallas_call(
        pack_kernel,
        name="pack",
        out_shape=(jax.ShapeDtypeStruct((4, ns), f32), jax.ShapeDtypeStruct((4, nt + width), f32)),
        in_specs=[SMEM] * 3 + [VMEM] * 8,
        out_specs=(VMEM, VMEM),
        compiler_params=pltpu.CompilerParams(vmem_limit_bytes=PACK_VMEM),
    )(asked, src_count, tgt_count, pair_src.reshape(1, -1), pair_slot.reshape(1, -1), *src_side, *tgt_side)

    src_in = [src_pack] + [moved(src_pack, "tgt", k) for k in range(1, n_tgt)]
    near = [tgt_pack] + [moved_inner(tgt_pack, "clus", k) for k in range(1, inner)]
    near = pl.pallas_call(
        join_kernel,
        name="join",
        out_shape=jax.ShapeDtypeStruct((4 * inner, nt + width), f32),
        in_specs=[VMEM] * inner,
        out_specs=VMEM,
        compiler_params=small,
    )(*near)
    tgt_in = {0: near, **{k: moved_outer(near, "clus", k) for cut in stages(outer)[1:] for k in cut}}

    block_rows = jax.ShapeDtypeStruct((n_src + 1, 8, BLK), f32)
    left_side = jax.ShapeDtypeStruct((n_src + 1, 32, BLK), jnp.bfloat16)
    n_pairs = pair_src.shape[0]
    memo_rows = jax.ShapeDtypeStruct((len(stages(outer)) * (1 + n_pairs) + slots, LANES), jnp.int32)
    list_scratch = (
        [pltpu.SMEM((n_pairs + 1,), jnp.int32)] * 2
        + [pltpu.VMEM((4, width), jnp.int32)]
    )
    kern_bufs = [pltpu.VMEM((GROUP, 2, BLK, BLK), jnp.bfloat16)] * BUFS
    part_shape = jax.ShapeDtypeStruct((inner, 4, per_req * BLK), f32)
    state, sums = (), {}
    for turn, mine in enumerate(stages(outer)):
        begins, ends = turn == 0, turn == len(stages(outer)) - 1
        held = [k for cut in stages(outer)[1:turn] for k in cut] if ends else []
        args = ([pair_count, me] + src_in if begins else list(state)) + [tgt_in[k] for k in mine] + [sums[k] for k in held]
        outs = [memo_rows, left_side, block_rows] if begins and not ends else []
        outs += [jax.ShapeDtypeStruct((4, ns), f32)] * n_tgt if ends else [block_rows]
        outs += [part_shape] * (len(mine) + len(held))
        extra = [pltpu.VMEM(block_rows.shape, f32)] if ends else []
        if begins and ends:
            extra += [pltpu.VMEM(memo_rows.shape, jnp.int32)]
            extra += [pltpu.VMEM(left_side.shape, jnp.bfloat16), pltpu.VMEM(block_rows.shape, f32)]
        extra += [
            pltpu.VMEM((slots, BLK, 32), jnp.bfloat16),
            pltpu.VMEM((slots, 8, BLK), f32),
            pltpu.VMEM((slots, 8, BLK), f32),
        ]
        res = pl.pallas_call(
            functools.partial(pairs_kernel, n_tgt, n_clus, per_req, turn),
            name=f"pairs_{turn}",
            out_shape=outs,
            in_specs=[SMEM if a is pair_count else ANY if a is me else VMEM for a in args],
            out_specs=[VMEM] * len(outs),
            scratch_shapes=extra + (list_scratch if begins else []) + kern_bufs,
            compiler_params=small,
            cost_estimate=pl.CostEstimate(flops=4*10**8 if begins else 0, bytes_accessed=2**20, transcendentals=0),
        )(*args)
        made = list(mine) + held
        sums.update(zip(made, res[len(res) - len(made) :]))
        if ends:
            src_out = res[:n_tgt]
        else:
            state = tuple(res[:4]) if begins else state[:3] + (res[0],)

    src_parts = [src_out[0]] + [moved(src_out[k], "tgt", k) for k in range(1, n_tgt)]
    tgt_parts = [sums[0]] + [moved_outer(sums[k], "clus", flip(k, outer)) for k in range(1, outer)]
    part_keep = functools.partial(
        pl.pallas_call,
        keep_kernel,
        name="keep",
        out_shape=part_shape,
        out_specs=VMEM,
        compiler_params=small,
    )
    for k in reversed(range(2, outer)):
        late = tgt_parts[k + 1 : k + 2]
        tgt_parts[k] = part_keep(in_specs=[VMEM] * (1 + len(late)))(tgt_parts[k], *late)
    if inner == 2:
        beside = pl.pallas_call(
            pick_kernel,
            name="pick",
            out_shape=jax.ShapeDtypeStruct((outer, 4, per_req * BLK), f32),
            in_specs=[VMEM] * outer,
            out_specs=VMEM,
            compiler_params=small,
        )(*tgt_parts)
        tgt_parts.append(moved_inner(beside, "clus", 1))

    grad_src_pos, grad_src_weight, ids, live = pl.pallas_call(
        functools.partial(src_kernel, n_tgt, per_req),
        name="finish_src",
        out_shape=(
            jax.ShapeDtypeStruct((3, ns), f32),
            jax.ShapeDtypeStruct((1, ns), f32),
            jax.ShapeDtypeStruct((slots, 4, BLK), f32),
            jax.ShapeDtypeStruct((1, nt), f32),
        ),
        in_specs=[SMEM] * 3 + [VMEM] * (3 + n_tgt + outer),
        out_specs=(VMEM,) * 4,
        compiler_params=small,
    )(me, src_count, tgt_count, *src_side, *src_parts, *(tgt_in[k] for k in range(outer)))
    grad_tgt_pos, grad_tgt_weight = pl.pallas_call(
        functools.partial(tgt_kernel, outer, inner),
        name="finish_tgt",
        out_shape=(jax.ShapeDtypeStruct((3, nt), f32), jax.ShapeDtypeStruct((1, nt), f32)),
        in_specs=[VMEM] * (5 + len(tgt_parts)),
        out_specs=(VMEM,) * 2,
        compiler_params=small,
    )(*tgt_side, live, ids, *tgt_parts)
    return grad_src_pos, grad_src_weight.reshape(-1), grad_tgt_pos, grad_tgt_weight.reshape(-1)


def solution(mesh):
    placed = (
        P(None, ("clus", "tgt")),
        P(("clus", "tgt")),
        P(("clus", "tgt")),
        P(("clus", "tgt")),
        P(None, ("clus", "tgt")),
        P(("clus", "tgt")),
        P(("clus", "tgt")),
        P(("clus", "tgt")),
        P(("clus", "tgt"), None),
        P(("clus", "tgt")),
        P(("clus", "tgt")),
        P(("clus", "tgt")),
    )
    return jax.shard_map(
        shards,
        mesh=mesh,
        in_specs=placed,
        out_specs=(
            P(None, ("clus", "tgt")),
            P(("clus", "tgt")),
            P(None, ("clus", "tgt")),
            P(("clus", "tgt")),
        ),
        check_vma=False,
    )
```

```python
import functools
import math

import jax
import jax.numpy as jnp
from jax import lax
from jax.experimental import pallas as pl
from jax.experimental.pallas import tpu as pltpu
from jax.sharding import PartitionSpec as P

BLK = 256
LANES = 128
GROUP = 2
BUFS = 4

entropic = 0.05
LOG2E = math.log2(math.e)
SCALE = LOG2E / entropic
DEAD = -4096.0
PACK_VMEM = 60 * 2**20
MAIN_VMEM = 24 * 2**20

VMEM = pl.BlockSpec(memory_space=pltpu.VMEM)
SMEM = pl.BlockSpec(memory_space=pltpu.SMEM)
ANY = pl.BlockSpec(memory_space=pl.ANY)


def divide(x, n):
    shift = n.bit_length() - 1
    return lax.shift_right_logical(x, jnp.int32(shift)) if n == 1 << shift else lax.div(x, jnp.int32(n))


def step(i, k, n):
    return i ^ k if n & (n - 1) == 0 else (i + k) % n


def back(i, k, n):
    return i ^ k if n & (n - 1) == 0 else (i + n - k) % n


def flip(k, n):
    return k if n & (n - 1) == 0 else (n - k) % n


def split_axis(n):
    inner = 2 if n % 2 == 0 else 1
    return n // inner, inner


def moved(x, axis, k):
    n = lax.axis_size(axis)
    return lax.ppermute(x, axis, [(i, step(i, k, n)) for i in range(n)])


def moved_outer(x, axis, k):
    outer, inner = split_axis(lax.axis_size(axis))
    pairs = [(o * inner + i, step(o, k, outer) * inner + i) for o in range(outer) for i in range(inner)]
    return lax.ppermute(x, axis, pairs)


def moved_inner(x, axis, k):
    outer, inner = split_axis(lax.axis_size(axis))
    pairs = [(o * inner + i, o * inner + step(i, k, inner)) for o in range(outer) for i in range(inner)]
    return lax.ppermute(x, axis, pairs)


def live_row(count_ref, block):
    lane = lax.broadcasted_iota(jnp.int32, (1, BLK), 1)
    return lane < count_ref[block]


def pack_side(pos_ref, weight_ref, pot_ref, count_ref, out_ref):
    for b in range(count_ref.shape[0]):
        cols = slice(b * BLK, (b + 1) * BLK)
        pos = pos_ref[:, cols]
        norm = jnp.sum(pos * pos, axis=0, keepdims=True)
        expo = (pot_ref[:, cols] - 0.5 * norm) * SCALE + jnp.log(weight_ref[:, cols]) * LOG2E
        out_ref[0:3, cols] = pos
        out_ref[3:4, cols] = jnp.where(live_row(count_ref, b), expo, DEAD)


def pack_kernel(req_ref, sc_ref, tc_ref, ps_ref, pq_ref, sp_ref, sw_ref, so_ref, tp_ref, tw_ref, to_ref, src_ref, tgt_ref):
    pack_side(sp_ref, sw_ref, so_ref, sc_ref, src_ref)
    pack_side(tp_ref, tw_ref, to_ref, tc_ref, tgt_ref)
    per, rows = req_ref.shape
    own = tp_ref.shape[1]
    lane = lax.broadcasted_iota(jnp.int32, (1, tgt_ref.shape[1] - own), 1)
    ids = jnp.zeros(lane.shape, jnp.float32)
    for r in range(rows):
        for m in range(per):
            ids = jnp.where(lane == r * per + m, req_ref[m, r].astype(jnp.float32), ids)
    tgt_ref[:, own:] = jnp.zeros((4,) + lane.shape[1:], jnp.float32)
    tgt_ref[0:1, own:] = ids
    tgt_ref[1:2, own : own + ps_ref.shape[1]] = ps_ref[...].astype(jnp.float32)
    tgt_ref[2:3, own : own + pq_ref.shape[1]] = pq_ref[...].astype(jnp.float32)


def split3(x):
    high = x.astype(jnp.bfloat16).astype(jnp.float32)
    rest = x - high
    mid = rest.astype(jnp.bfloat16).astype(jnp.float32)
    return high, mid, rest - mid


def stages(outer):
    cuts = [(0, 1), (outer - 1, outer), (1, outer - 1)]
    return [(first, stop) for i, (first, stop) in enumerate(cuts) if first < stop and (i == 0 or first > 0)]


def dot(x, y):
    return jnp.dot(x, y, preferred_element_type=jnp.float32)


def dot_t(x, y):
    return lax.dot_general(x, y, (((1,), (1,)), ((), ())), preferred_element_type=jnp.float32)


def away(i, me, n):
    return i ^ me if n & (n - 1) == 0 else lax.rem(me - i + n, n)


def is_power(n):
    return n & (n - 1) == 0


def local_block(s, me, n, per_dev):
    if is_power(n) and is_power(per_dev):
        return s ^ (me * per_dev)
    dev = divide(s, per_dev)
    return s + (away(dev, me, n) - dev) * per_dev


def local_slot(q, outer_me, inner_me, outer, inner, per_req):
    if is_power(outer) and is_power(inner) and is_power(per_req):
        return q ^ ((outer_me * inner + inner_me) * per_req)
    clus = divide(q, per_req)
    place = divide(clus, inner)
    side = away(clus - place * inner, inner_me, inner)
    return (away(place, outer_me, outer) * inner + side - clus) * per_req + q


def prepare_src(src_in, left, src_rows):
    last = lax.broadcasted_iota(jnp.int32, (4, BLK), 0) == 3
    pad = jnp.zeros((8, BLK), jnp.float32)
    per_dev = src_in[0].shape[1] // BLK
    for k, part in enumerate(src_in):
        for b in range(per_dev):
            high, mid, low = split3(part[:, b * BLK : (b + 1) * BLK])
            high1, mid1 = jnp.where(last, 1.0, high), jnp.where(last, 1.0, mid)
            place = k * per_dev + b
            left[place] = jnp.concatenate([high, high1, high1, mid, mid1, low, pad], 0).astype(jnp.bfloat16)
            src_rows[place] = jnp.concatenate([high1, jnp.where(last, 0.0, mid)], 0)
    dead = lax.broadcasted_iota(jnp.int32, (32, BLK), 0) == 3
    left[len(src_in) * per_dev] = jnp.where(dead, DEAD, 0.0).astype(jnp.bfloat16)
    src_rows[len(src_in) * per_dev] = pad


def prepare_tgt(slot, block, rows, tgt_in, right, tgt_rows):
    last = lax.broadcasted_iota(jnp.int32, (4, BLK), 0) == 3
    pad = jnp.zeros((8, BLK), jnp.float32)
    raw = tgt_in[rows, pl.ds(pl.multiple_of(block * BLK, BLK), BLK)]
    high, mid, _ = split3(raw)
    tgt_rows[slot] = jnp.concatenate([jnp.where(last, 1.0, high), jnp.where(last, 0.0, mid)], 0)
    high, mid, low = split3(jnp.where(last, raw, raw * SCALE))
    high1 = jnp.where(last, 1.0, high)
    wide = jnp.concatenate([high1, mid, low, high1, jnp.where(last, high, mid), high1, pad], 0)
    right[slot] = wide.T.astype(jnp.bfloat16)


def pairs_kernel(n_tgt, n_clus, per_req, turn, *refs):
    outer, inner = split_axis(n_clus)
    cuts = stages(outer)
    first, stop = cuts[turn]
    begins, ends = turn == 0, turn == len(cuts) - 1
    slots = n_clus * per_req
    refs = list(refs)
    take = lambda n: [refs.pop(0) for _ in range(n)]
    if begins:
        (far_me,) = take(1)
        src_in = take(n_tgt)
    else:
        memo, left, src_rows, src_sums = take(4)
    tgt_in = take(stop - first)
    held = [k for cut in cuts[1:turn] for k in range(*cut)] if ends else []
    held_in = take(len(held))
    if begins and not ends:
        memo, left, src_rows = take(3)
    src_out = take(n_tgt if ends else 1)
    tgt_out = take(stop - first)
    for far, near in zip(held_in, take(len(held))):
        near[...] = far[...]
    src_acc = take(1)[0] if ends else src_out[0]
    if begins and ends:
        memo, left, src_rows = take(3)
    right, tgt_rows, tgt_acc, *refs = refs
    if begins:
        (chosen_src, chosen_slot, sem, me_ref, head), kern_bufs = refs[:5], refs[5:]
        copy = pltpu.make_async_copy(far_me, me_ref, sem)
        copy.start()
        head[...] = tgt_in[0][0:4, tgt_in[0].shape[1] - head.shape[1] :].astype(jnp.int32)
    else:
        kern_bufs = refs
    n_src = left.shape[0] - 1
    per_dev = n_src // n_tgt
    if begins:
        prepare_src(src_in, left, src_rows)
        src_acc[...] = jnp.zeros_like(src_acc)
    else:
        src_acc[...] = src_sums[...]
    tgt_acc[...] = jnp.zeros_like(tgt_acc)

    pairs = (memo.shape[0] - len(cuts) - slots) // (2 * len(cuts))
    tops = [len(cuts) + slots + 2 * pairs * i for i in range(len(cuts))]

    def note(row, value):
        memo[pl.ds(row, 1), :] = jnp.full((1, LANES), value, jnp.int32)

    if begins:
        copy.wait()
        tgt_me, outer_me, inner_me, count = (me_ref[i] for i in range(4))
        for slot in range(slots):
            note(len(cuts) + local_slot(slot, outer_me, inner_me, outer, inner, per_req), head[0, slot])
        totals = [jnp.int32(0)] * len(cuts)
        for pair in range(pairs):
            s = local_block(head[1, pair], tgt_me, n_tgt, per_dev)
            slot = local_slot(head[2, pair], outer_me, inner_me, outer, inner, per_req)
            for i, (low, high) in enumerate(cuts):
                inside = slot - low * inner * per_req
                if i == 0:
                    chosen_src[totals[0]] = s
                    chosen_slot[totals[0]] = inside
                else:
                    note(tops[i] + totals[i], s)
                    note(tops[i] + pairs + totals[i], inside)
                hit = (pair < count) & (inside >= 0) & (inside < (high - low) * inner * per_req)
                totals[i] = totals[i] + hit.astype(jnp.int32)
        for i in range(1, len(cuts)):
            note(i, totals[i])
        total = totals[0]
    else:
        total = memo[turn, 0]
    for slot in range((stop - first) * inner * per_req):
        i = slot // per_req % inner
        block = memo[len(cuts) + first * inner * per_req + slot, 0]
        prepare_tgt(slot, block, slice(4 * i, 4 * i + 4), tgt_in[slot // (inner * per_req)], right, tgt_rows)

    def pair_ids(entry):
        inside = jnp.minimum(entry, pairs - 1)
        live = entry < total
        if begins:
            s, q = chosen_src[inside], chosen_slot[inside]
        else:
            s, q = memo[tops[turn] + inside, 0], memo[tops[turn] + pairs + inside, 0]
        return jnp.where(live, s, n_src), jnp.where(live, q, 0)

    def weigh(entry, buf, g):
        s, q = pair_ids(entry)
        kern = jnp.exp2(dot(right[q], left[s]))
        high = kern.astype(jnp.bfloat16)
        buf[g, 0] = high
        buf[g, 1] = (kern - high.astype(jnp.float32)).astype(jnp.bfloat16)

    def reduce(entry, buf, g):
        s, q = pair_ids(entry)
        high, low = buf[g, 0], buf[g, 1]
        y = tgt_rows[q].astype(jnp.bfloat16)
        x = src_rows[s].astype(jnp.bfloat16)
        tgt_part = dot_t(x, high) + dot_t(x, low)
        return s, q, dot(y, high) + dot(y, low), tgt_part

    bufs = len(kern_bufs)
    for g in range(GROUP):
        weigh(g, kern_bufs[0], g)

    def body(trip, carry):
        start = trip * bufs * GROUP
        for u in range(bufs):
            parts = []
            for g in range(GROUP):
                weigh(start + (u + 1) * GROUP + g, kern_bufs[(u + 1) % bufs], g)
                parts.append(reduce(start + u * GROUP + g, kern_bufs[u], g))
            for s, q, src_part, tgt_part in parts:
                src_acc[s] += src_part
                tgt_acc[q] += tgt_part
        return carry

    lax.fori_loop(0, divide(total + GROUP * bufs - 1, GROUP * bufs), body, 0)

    for place in range((stop - first) * inner):
        for m in range(per_req):
            part = tgt_acc[place * per_req + m]
            tgt_out[place // inner][place % inner, :, m * BLK : (m + 1) * BLK] = part[0:4] + part[4:8]
    if ends:
        for k in range(n_tgt):
            base = flip(k, n_tgt) * per_dev
            for b in range(per_dev):
                part = src_acc[base + b]
                src_out[k][:, b * BLK : (b + 1) * BLK] = part[0:4] + part[4:8]


def join_kernel(*refs):
    *parts, out_ref = refs
    for k, part in enumerate(parts):
        out_ref[4 * k : 4 * k + 4] = part[...]


def keep_kernel(*refs):
    refs[-1][...] = refs[0][...]


def pick_kernel(*refs):
    *parts, out_ref = refs
    for k, part in enumerate(parts):
        out_ref[k] = part[1]


def finish_side(pos, weight, pot, live, total):
    mass = total[3:4]
    return pos * mass - total[0:3], jnp.where(live, pot - entropic * mass / weight, 0.0)


def src_kernel(n_tgt, per_req, me_ref, src_count_ref, tgt_count_ref, pos_ref, weight_ref, pot_ref, *refs):
    parts, refs = refs[:n_tgt], refs[n_tgt:]
    *tgt_in, grad_pos_ref, grad_weight_ref, ids_ref, live_ref = refs
    for b in range(src_count_ref.shape[0]):
        cols = slice(b * BLK, (b + 1) * BLK)
        grad_pos_ref[:, cols], grad_weight_ref[:, cols] = finish_side(
            pos_ref[:, cols],
            weight_ref[:, cols],
            pot_ref[:, cols],
            live_row(src_count_ref, b),
            sum(p[:, cols] for p in parts),
        )
    for b in range(tgt_count_ref.shape[0]):
        live_ref[:, b * BLK : (b + 1) * BLK] = live_row(tgt_count_ref, b).astype(jnp.float32)
    outer = len(tgt_in)
    inner = tgt_in[0].shape[0] // 4
    outer_me, inner_me = me_ref[1], me_ref[2]
    me = outer_me * inner + inner_me
    own = tgt_count_ref.shape[0] * BLK
    width = tgt_in[0].shape[1] - own
    lane = lax.broadcasted_iota(jnp.int32, (1, width), 1)
    for k in range(outer):
        for i in range(inner):
            row = tgt_in[flip(k, outer)][4 * i : 4 * i + 1, own:]
            for m in range(per_req):
                block = jnp.sum(jnp.where(lane == me * per_req + m, row, 0.0), axis=1, keepdims=True)
                ids_ref[(k * inner + i) * per_req + m] = jnp.broadcast_to(block, (4, BLK))


def tgt_kernel(outer, inner, pos_ref, weight_ref, pot_ref, live_ref, ids_ref, *refs):
    *parts, grad_pos_ref, grad_weight_ref = refs
    own, side = parts[:outer], parts[outer:]
    per_req = ids_ref.shape[0] // (outer * inner)
    for b in range(pos_ref.shape[1] // BLK):
        cols = slice(b * BLK, (b + 1) * BLK)
        total = jnp.zeros((4, BLK), jnp.float32)
        for k in range(outer):
            for i in range(inner):
                for m in range(per_req):
                    wide = slice(m * BLK, (m + 1) * BLK)
                    part = own[k][0, :, wide] if i == 0 else side[i - 1][k, :, wide]
                    total += jnp.where(ids_ref[(k * inner + i) * per_req + m] == b, part, 0.0)
        grad_pos_ref[:, cols], grad_weight_ref[:, cols] = finish_side(
            pos_ref[:, cols], weight_ref[:, cols], pot_ref[:, cols], live_ref[:, cols] > 0.0, total
        )


def shards(
    src_pos,
    src_weight,
    src_pot,
    src_count,
    tgt_pos,
    tgt_weight,
    tgt_pot,
    tgt_count,
    requests,
    pair_src,
    pair_slot,
    pair_count,
):
    f32 = jnp.float32
    n_tgt, n_clus = lax.axis_size("tgt"), lax.axis_size("clus")
    outer, inner = split_axis(n_clus)
    ns, nt = src_pos.shape[1], tgt_pos.shape[1]
    n_src = n_tgt * (ns // BLK)
    per_req = requests.shape[1]
    slots = n_clus * per_req
    width = -(-max(slots, pair_src.shape[0]) // LANES) * LANES
    asked = requests.T
    small = pltpu.CompilerParams(vmem_limit_bytes=MAIN_VMEM)
    clus_me = lax.axis_index("clus")
    me = jnp.stack([lax.axis_index("tgt"), clus_me // inner, clus_me % inner, pair_count[0]]).astype(jnp.int32)
    src_side = (src_pos, src_weight.reshape(1, -1), src_pot.reshape(1, -1))
    tgt_side = (tgt_pos, tgt_weight.reshape(1, -1), tgt_pot.reshape(1, -1))

    src_pack, tgt_pack = pl.pallas_call(
        pack_kernel,
        name="pack",
        out_shape=(jax.ShapeDtypeStruct((4, ns), f32), jax.ShapeDtypeStruct((4, nt + width), f32)),
        in_specs=[SMEM] * 3 + [VMEM] * 8,
        out_specs=(VMEM, VMEM),
        compiler_params=pltpu.CompilerParams(vmem_limit_bytes=PACK_VMEM),
    )(asked, src_count, tgt_count, pair_src.reshape(1, -1), pair_slot.reshape(1, -1), *src_side, *tgt_side)

    src_in = [src_pack] + [moved(src_pack, "tgt", k) for k in range(1, n_tgt)]
    near = [tgt_pack] + [moved_inner(tgt_pack, "clus", k) for k in range(1, inner)]
    near = pl.pallas_call(
        join_kernel,
        name="join",
        out_shape=jax.ShapeDtypeStruct((4 * inner, nt + width), f32),
        in_specs=[VMEM] * inner,
        out_specs=VMEM,
        compiler_params=small,
    )(*near)
    tgt_in = [near] + [moved_outer(near, "clus", k) for k in range(1, outer)]

    block_rows = jax.ShapeDtypeStruct((n_src + 1, 8, BLK), f32)
    left_side = jax.ShapeDtypeStruct((n_src + 1, 32, BLK), jnp.bfloat16)
    n_pairs = pair_src.shape[0]
    memo_rows = jax.ShapeDtypeStruct((len(stages(outer)) * (1 + 2 * n_pairs) + slots, LANES), jnp.int32)
    list_scratch = (
        [pltpu.SMEM((n_pairs + 1,), jnp.int32)] * 2
        + [pltpu.SemaphoreType.DMA, pltpu.SMEM(me.shape, jnp.int32)]
        + [pltpu.VMEM((4, width), jnp.int32)]
    )
    kern_bufs = [pltpu.VMEM((GROUP, 2, BLK, BLK), jnp.bfloat16)] * BUFS
    part_shape = jax.ShapeDtypeStruct((inner, 4, per_req * BLK), f32)
    state, sums = (), {}
    for turn, (first, stop) in enumerate(stages(outer)):
        begins, ends = turn == 0, turn == len(stages(outer)) - 1
        held = [k for cut in stages(outer)[1:turn] for k in range(*cut)] if ends else []
        args = ([me] + src_in if begins else list(state)) + tgt_in[first:stop] + [sums[k] for k in held]
        outs = [memo_rows, left_side, block_rows] if begins and not ends else []
        outs += [jax.ShapeDtypeStruct((4, ns), f32)] * n_tgt if ends else [block_rows]
        outs += [part_shape] * (stop - first + len(held))
        extra = [pltpu.VMEM(block_rows.shape, f32)] if ends else []
        if begins and ends:
            extra += [pltpu.VMEM(memo_rows.shape, jnp.int32)]
            extra += [pltpu.VMEM(left_side.shape, jnp.bfloat16), pltpu.VMEM(block_rows.shape, f32)]
        near = (stop - first) * inner * per_req
        extra += [
            pltpu.VMEM((near, BLK, 32), jnp.bfloat16),
            pltpu.VMEM((near, 8, BLK), f32),
            pltpu.VMEM((near, 8, BLK), f32),
        ]
        res = pl.pallas_call(
            functools.partial(pairs_kernel, n_tgt, n_clus, per_req, turn),
            name=f"pairs_{first}_{stop}",
            out_shape=outs,
            in_specs=[ANY if begins and a is me else VMEM for a in args],
            out_specs=[VMEM] * len(outs),
            scratch_shapes=extra + (list_scratch if begins else []) + kern_bufs,
            compiler_params=small,
            cost_estimate=pl.CostEstimate(flops=4*10**8 if begins else 0, bytes_accessed=2**20, transcendentals=0),
        )(*args)
        made = list(range(first, stop)) + held
        sums.update(zip(made, res[len(res) - len(made) :]))
        if ends:
            src_out = res[:n_tgt]
        else:
            state = tuple(res[:4]) if begins else state[:3] + (res[0],)

    src_parts = [src_out[0]] + [moved(src_out[k], "tgt", k) for k in range(1, n_tgt)]
    tgt_parts = [sums[0]] + [moved_outer(sums[k], "clus", flip(k, outer)) for k in range(1, outer)]
    part_keep = functools.partial(
        pl.pallas_call,
        keep_kernel,
        name="keep",
        out_shape=part_shape,
        out_specs=VMEM,
        compiler_params=small,
    )
    for k in reversed(range(2, outer)):
        late = tgt_parts[k + 1 : k + 2]
        tgt_parts[k] = part_keep(in_specs=[VMEM] * (1 + len(late)))(tgt_parts[k], *late)
    if inner == 2:
        beside = pl.pallas_call(
            pick_kernel,
            name="pick",
            out_shape=jax.ShapeDtypeStruct((outer, 4, per_req * BLK), f32),
            in_specs=[VMEM] * outer,
            out_specs=VMEM,
            compiler_params=small,
        )(*tgt_parts)
        tgt_parts.append(moved_inner(beside, "clus", 1))

    grad_src_pos, grad_src_weight, ids, live = pl.pallas_call(
        functools.partial(src_kernel, n_tgt, per_req),
        name="finish_src",
        out_shape=(
            jax.ShapeDtypeStruct((3, ns), f32),
            jax.ShapeDtypeStruct((1, ns), f32),
            jax.ShapeDtypeStruct((slots, 4, BLK), f32),
            jax.ShapeDtypeStruct((1, nt), f32),
        ),
        in_specs=[SMEM] * 3 + [VMEM] * (3 + n_tgt + outer),
        out_specs=(VMEM,) * 4,
        compiler_params=small,
    )(me, src_count, tgt_count, *src_side, *src_parts, *tgt_in)
    grad_tgt_pos, grad_tgt_weight = pl.pallas_call(
        functools.partial(tgt_kernel, outer, inner),
        name="finish_tgt",
        out_shape=(jax.ShapeDtypeStruct((3, nt), f32), jax.ShapeDtypeStruct((1, nt), f32)),
        in_specs=[VMEM] * (5 + len(tgt_parts)),
        out_specs=(VMEM,) * 2,
        compiler_params=small,
    )(*tgt_side, live, ids, *tgt_parts)
    return grad_src_pos, grad_src_weight.reshape(-1), grad_tgt_pos, grad_tgt_weight.reshape(-1)


def solution(mesh):
    placed = (
        P(None, ("clus", "tgt")),
        P(("clus", "tgt")),
        P(("clus", "tgt")),
        P(("clus", "tgt")),
        P(None, ("clus", "tgt")),
        P(("clus", "tgt")),
        P(("clus", "tgt")),
        P(("clus", "tgt")),
        P(("clus", "tgt"), None),
        P(("clus", "tgt")),
        P(("clus", "tgt")),
        P(("clus", "tgt")),
    )
    return jax.shard_map(
        shards,
        mesh=mesh,
        in_specs=placed,
        out_specs=(
            P(None, ("clus", "tgt")),
            P(("clus", "tgt")),
            P(None, ("clus", "tgt")),
            P(("clus", "tgt")),
        ),
        check_vma=False,
    )
```

```python
import functools
import math

import jax
import jax.numpy as jnp
from jax import lax
from jax.experimental import pallas as pl
from jax.experimental.pallas import tpu as pltpu
from jax.sharding import PartitionSpec as P

BLK = 256
LANES = 128
GROUP = 2
BUFS = 4

entropic = 0.05
LOG2E = math.log2(math.e)
SCALE = LOG2E / entropic
DEAD = -4096.0
PACK_VMEM = 60 * 2**20
MAIN_VMEM = 24 * 2**20

VMEM = pl.BlockSpec(memory_space=pltpu.VMEM)
SMEM = pl.BlockSpec(memory_space=pltpu.SMEM)
ANY = pl.BlockSpec(memory_space=pl.ANY)


def divide(x, n):
    shift = n.bit_length() - 1
    return lax.shift_right_logical(x, jnp.int32(shift)) if n == 1 << shift else lax.div(x, jnp.int32(n))


def step(i, k, n):
    return i ^ k if n & (n - 1) == 0 else (i + k) % n


def back(i, k, n):
    return i ^ k if n & (n - 1) == 0 else (i + n - k) % n


def flip(k, n):
    return k if n & (n - 1) == 0 else (n - k) % n


def split_axis(n):
    inner = 2 if n % 2 == 0 else 1
    return n // inner, inner


def moved(x, axis, k):
    n = lax.axis_size(axis)
    return lax.ppermute(x, axis, [(i, step(i, k, n)) for i in range(n)])


def moved_outer(x, axis, k):
    outer, inner = split_axis(lax.axis_size(axis))
    pairs = [(o * inner + i, step(o, k, outer) * inner + i) for o in range(outer) for i in range(inner)]
    return lax.ppermute(x, axis, pairs)


def moved_inner(x, axis, k):
    outer, inner = split_axis(lax.axis_size(axis))
    pairs = [(o * inner + i, o * inner + step(i, k, inner)) for o in range(outer) for i in range(inner)]
    return lax.ppermute(x, axis, pairs)


def live_row(count_ref, block):
    lane = lax.broadcasted_iota(jnp.int32, (1, BLK), 1)
    return lane < count_ref[block]


def pack_side(pos_ref, weight_ref, pot_ref, count_ref, out_ref):
    for b in range(count_ref.shape[0]):
        cols = slice(b * BLK, (b + 1) * BLK)
        pos = pos_ref[:, cols]
        norm = jnp.sum(pos * pos, axis=0, keepdims=True)
        expo = (pot_ref[:, cols] - 0.5 * norm) * SCALE + jnp.log(weight_ref[:, cols]) * LOG2E
        out_ref[0:3, cols] = pos
        out_ref[3:4, cols] = jnp.where(live_row(count_ref, b), expo, DEAD)


def pack_kernel(req_ref, sc_ref, tc_ref, ps_ref, pq_ref, sp_ref, sw_ref, so_ref, tp_ref, tw_ref, to_ref, src_ref, tgt_ref):
    pack_side(sp_ref, sw_ref, so_ref, sc_ref, src_ref)
    pack_side(tp_ref, tw_ref, to_ref, tc_ref, tgt_ref)
    per, rows = req_ref.shape
    own = tp_ref.shape[1]
    lane = lax.broadcasted_iota(jnp.int32, (1, tgt_ref.shape[1] - own), 1)
    ids = jnp.zeros(lane.shape, jnp.float32)
    for r in range(rows):
        for m in range(per):
            ids = jnp.where(lane == r * per + m, req_ref[m, r].astype(jnp.float32), ids)
    tgt_ref[:, own:] = jnp.zeros((4,) + lane.shape[1:], jnp.float32)
    tgt_ref[0:1, own:] = ids
    tgt_ref[1:2, own : own + ps_ref.shape[1]] = ps_ref[...].astype(jnp.float32)
    tgt_ref[2:3, own : own + pq_ref.shape[1]] = pq_ref[...].astype(jnp.float32)


def split3(x):
    high = x.astype(jnp.bfloat16).astype(jnp.float32)
    rest = x - high
    mid = rest.astype(jnp.bfloat16).astype(jnp.float32)
    return high, mid, rest - mid


def stages(outer):
    cuts = [(0, 1), (outer - 1, outer), (1, outer - 1)]
    return [(first, stop) for i, (first, stop) in enumerate(cuts) if first < stop and (i == 0 or first > 0)]


def dot(x, y):
    return jnp.dot(x, y, preferred_element_type=jnp.float32)


def dot_t(x, y):
    return lax.dot_general(x, y, (((1,), (1,)), ((), ())), preferred_element_type=jnp.float32)


def away(i, me, n):
    return i ^ me if n & (n - 1) == 0 else lax.rem(me - i + n, n)


def is_power(n):
    return n & (n - 1) == 0


def local_block(s, me, n, per_dev):
    if is_power(n) and is_power(per_dev):
        return s ^ (me * per_dev)
    dev = divide(s, per_dev)
    return s + (away(dev, me, n) - dev) * per_dev


def local_slot(q, outer_me, inner_me, outer, inner, per_req):
    if is_power(outer) and is_power(inner) and is_power(per_req):
        return q ^ ((outer_me * inner + inner_me) * per_req)
    clus = divide(q, per_req)
    place = divide(clus, inner)
    side = away(clus - place * inner, inner_me, inner)
    return (away(place, outer_me, outer) * inner + side - clus) * per_req + q


def prepare_src(src_in, left, src_rows):
    last = lax.broadcasted_iota(jnp.int32, (4, BLK), 0) == 3
    pad = jnp.zeros((8, BLK), jnp.float32)
    per_dev = src_in[0].shape[1] // BLK
    for k, part in enumerate(src_in):
        for b in range(per_dev):
            high, mid, low = split3(part[:, b * BLK : (b + 1) * BLK])
            high1, mid1 = jnp.where(last, 1.0, high), jnp.where(last, 1.0, mid)
            place = k * per_dev + b
            left[place] = jnp.concatenate([high, high1, high1, mid, mid1, low, pad], 0).astype(jnp.bfloat16)
            src_rows[place] = jnp.concatenate([high1, jnp.where(last, 0.0, mid)], 0)
    dead = lax.broadcasted_iota(jnp.int32, (32, BLK), 0) == 3
    left[len(src_in) * per_dev] = jnp.where(dead, DEAD, 0.0).astype(jnp.bfloat16)
    src_rows[len(src_in) * per_dev] = pad


def prepare_tgt(slot, block, rows, tgt_in, right, tgt_rows):
    last = lax.broadcasted_iota(jnp.int32, (4, BLK), 0) == 3
    pad = jnp.zeros((8, BLK), jnp.float32)
    raw = tgt_in[rows, pl.ds(pl.multiple_of(block * BLK, BLK), BLK)]
    high, mid, _ = split3(raw)
    tgt_rows[slot] = jnp.concatenate([jnp.where(last, 1.0, high), jnp.where(last, 0.0, mid)], 0)
    high, mid, low = split3(jnp.where(last, raw, raw * SCALE))
    high1 = jnp.where(last, 1.0, high)
    wide = jnp.concatenate([high1, mid, low, high1, jnp.where(last, high, mid), high1, pad], 0)
    right[slot] = wide.T.astype(jnp.bfloat16)


def pairs_kernel(n_tgt, n_clus, per_req, turn, *refs):
    outer, inner = split_axis(n_clus)
    cuts = stages(outer)
    first, stop = cuts[turn]
    begins, ends = turn == 0, turn == len(cuts) - 1
    slots = n_clus * per_req
    refs = list(refs)
    take = lambda n: [refs.pop(0) for _ in range(n)]
    if begins:
        (far_me,) = take(1)
        src_in = take(n_tgt)
    else:
        memo, left, src_rows, src_sums = take(4)
    tgt_in = take(stop - first)
    held = [k for cut in cuts[1:turn] for k in range(*cut)] if ends else []
    held_in = take(len(held))
    if begins and not ends:
        memo, left, src_rows = take(3)
    src_out = take(n_tgt if ends else 1)
    tgt_out = take(stop - first)
    for far, near in zip(held_in, take(len(held))):
        near[...] = far[...]
    src_acc = take(1)[0] if ends else src_out[0]
    if begins and ends:
        memo, left, src_rows = take(3)
    right, tgt_rows, tgt_acc, *refs = refs
    if begins:
        (chosen_src, chosen_slot, sem, me_ref, head), kern_bufs = refs[:5], refs[5:]
        copy = pltpu.make_async_copy(far_me, me_ref, sem)
        copy.start()
        head[...] = tgt_in[0][0:4, tgt_in[0].shape[1] - head.shape[1] :].astype(jnp.int32)
    else:
        kern_bufs = refs
    n_src = left.shape[0] - 1
    per_dev = n_src // n_tgt
    if begins:
        prepare_src(src_in, left, src_rows)
        src_acc[...] = jnp.zeros_like(src_acc)
    else:
        src_acc[...] = src_sums[...]
    tgt_acc[...] = jnp.zeros_like(tgt_acc)

    pairs = (memo.shape[0] - len(cuts) - slots) // (2 * len(cuts))
    tops = [len(cuts) + slots + 2 * pairs * i for i in range(len(cuts))]

    def note(row, value):
        memo[pl.ds(row, 1), :] = jnp.full((1, LANES), value, jnp.int32)

    if begins:
        copy.wait()
        tgt_me, outer_me, inner_me, count = (me_ref[i] for i in range(4))
        for slot in range(slots):
            note(len(cuts) + local_slot(slot, outer_me, inner_me, outer, inner, per_req), head[0, slot])
        totals = [jnp.int32(0)] * len(cuts)
        for pair in range(pairs):
            s = local_block(head[1, pair], tgt_me, n_tgt, per_dev)
            slot = local_slot(head[2, pair], outer_me, inner_me, outer, inner, per_req)
            for i, (low, high) in enumerate(cuts):
                inside = slot - low * inner * per_req
                if i == 0:
                    chosen_src[totals[0]] = s
                    chosen_slot[totals[0]] = inside
                else:
                    note(tops[i] + totals[i], s)
                    note(tops[i] + pairs + totals[i], inside)
                hit = (pair < count) & (inside >= 0) & (inside < (high - low) * inner * per_req)
                totals[i] = totals[i] + hit.astype(jnp.int32)
        for i in range(1, len(cuts)):
            note(i, totals[i])
        total = totals[0]
    else:
        total = memo[turn, 0]
    for slot in range((stop - first) * inner * per_req):
        i = slot // per_req % inner
        block = memo[len(cuts) + first * inner * per_req + slot, 0]
        prepare_tgt(slot, block, slice(4 * i, 4 * i + 4), tgt_in[slot // (inner * per_req)], right, tgt_rows)

    def pair_ids(entry):
        inside = jnp.minimum(entry, pairs - 1)
        live = entry < total
        if begins:
            s, q = chosen_src[inside], chosen_slot[inside]
        else:
            s, q = memo[tops[turn] + inside, 0], memo[tops[turn] + pairs + inside, 0]
        return jnp.where(live, s, n_src), jnp.where(live, q, 0)

    def weigh(entry, buf, g, rows=slice(0, BLK)):
        s, q = pair_ids(entry)
        kern = jnp.exp2(dot(right[q, rows], left[s]))
        high = kern.astype(jnp.bfloat16)
        buf[g, 0, rows] = high
        buf[g, 1, rows] = (kern - high.astype(jnp.float32)).astype(jnp.bfloat16)

    def reduce(entry, buf, g, ahead):
        s, q = pair_ids(entry)
        y = tgt_rows[q].astype(jnp.bfloat16)
        x = src_rows[s].astype(jnp.bfloat16)
        steps = [
            lambda: dot(y, buf[g, 0]),
            lambda: dot_t(x, buf[g, 0]),
            lambda: dot(y, buf[g, 1]),
            lambda: dot_t(x, buf[g, 1]),
        ]
        got = {}
        for i in (1, 3, 0, 2):
            for j, rows in ((0, slice(0, 256, None)),):
                if j == len(got):
                    ahead(rows)
            got[i] = steps[i]()
        return s, q, got[0] + got[2], got[1] + got[3]

    bufs = len(kern_bufs)
    for g in range(GROUP):
        weigh(g, kern_bufs[0], g)

    def body(trip, carry):
        start = trip * bufs * GROUP
        for u in range(bufs):
            parts = []
            for g in range(GROUP):
                ahead = functools.partial(weigh, start + (u + 1) * GROUP + g, kern_bufs[(u + 1) % bufs], g)
                parts.append(reduce(start + u * GROUP + g, kern_bufs[u], g, ahead))
            for s, q, src_part, tgt_part in parts:
                src_acc[s] += src_part
                tgt_acc[q] += tgt_part
        return carry

    lax.fori_loop(0, divide(total + GROUP * bufs - 1, GROUP * bufs), body, 0)

    for place in range((stop - first) * inner):
        for m in range(per_req):
            part = tgt_acc[place * per_req + m]
            tgt_out[place // inner][place % inner, :, m * BLK : (m + 1) * BLK] = part[0:4] + part[4:8]
    if ends:
        for k in range(n_tgt):
            base = flip(k, n_tgt) * per_dev
            for b in range(per_dev):
                part = src_acc[base + b]
                src_out[k][:, b * BLK : (b + 1) * BLK] = part[0:4] + part[4:8]


def join_kernel(*refs):
    *parts, out_ref = refs
    for k, part in enumerate(parts):
        out_ref[4 * k : 4 * k + 4] = part[...]


def keep_kernel(*refs):
    refs[-1][...] = refs[0][...]


def pick_kernel(*refs):
    *parts, out_ref = refs
    for k, part in enumerate(parts):
        out_ref[k] = part[1]


def finish_side(pos, weight, pot, live, total):
    mass = total[3:4]
    return pos * mass - total[0:3], jnp.where(live, pot - entropic * mass / weight, 0.0)


def src_kernel(n_tgt, per_req, me_ref, src_count_ref, tgt_count_ref, pos_ref, weight_ref, pot_ref, *refs):
    parts, refs = refs[:n_tgt], refs[n_tgt:]
    *tgt_in, grad_pos_ref, grad_weight_ref, ids_ref, live_ref = refs
    for b in range(src_count_ref.shape[0]):
        cols = slice(b * BLK, (b + 1) * BLK)
        grad_pos_ref[:, cols], grad_weight_ref[:, cols] = finish_side(
            pos_ref[:, cols],
            weight_ref[:, cols],
            pot_ref[:, cols],
            live_row(src_count_ref, b),
            sum(p[:, cols] for p in parts),
        )
    for b in range(tgt_count_ref.shape[0]):
        live_ref[:, b * BLK : (b + 1) * BLK] = live_row(tgt_count_ref, b).astype(jnp.float32)
    outer = len(tgt_in)
    inner = tgt_in[0].shape[0] // 4
    outer_me, inner_me = me_ref[1], me_ref[2]
    me = outer_me * inner + inner_me
    own = tgt_count_ref.shape[0] * BLK
    width = tgt_in[0].shape[1] - own
    lane = lax.broadcasted_iota(jnp.int32, (1, width), 1)
    for k in range(outer):
        for i in range(inner):
            row = tgt_in[flip(k, outer)][4 * i : 4 * i + 1, own:]
            for m in range(per_req):
                block = jnp.sum(jnp.where(lane == me * per_req + m, row, 0.0), axis=1, keepdims=True)
                ids_ref[(k * inner + i) * per_req + m] = jnp.broadcast_to(block, (4, BLK))


def tgt_kernel(outer, inner, pos_ref, weight_ref, pot_ref, live_ref, ids_ref, *refs):
    *parts, grad_pos_ref, grad_weight_ref = refs
    own, side = parts[:outer], parts[outer:]
    per_req = ids_ref.shape[0] // (outer * inner)
    for b in range(pos_ref.shape[1] // BLK):
        cols = slice(b * BLK, (b + 1) * BLK)
        total = jnp.zeros((4, BLK), jnp.float32)
        for k in range(outer):
            for i in range(inner):
                for m in range(per_req):
                    wide = slice(m * BLK, (m + 1) * BLK)
                    part = own[k][0, :, wide] if i == 0 else side[i - 1][k, :, wide]
                    total += jnp.where(ids_ref[(k * inner + i) * per_req + m] == b, part, 0.0)
        grad_pos_ref[:, cols], grad_weight_ref[:, cols] = finish_side(
            pos_ref[:, cols], weight_ref[:, cols], pot_ref[:, cols], live_ref[:, cols] > 0.0, total
        )


def shards(
    src_pos,
    src_weight,
    src_pot,
    src_count,
    tgt_pos,
    tgt_weight,
    tgt_pot,
    tgt_count,
    requests,
    pair_src,
    pair_slot,
    pair_count,
):
    f32 = jnp.float32
    n_tgt, n_clus = lax.axis_size("tgt"), lax.axis_size("clus")
    outer, inner = split_axis(n_clus)
    ns, nt = src_pos.shape[1], tgt_pos.shape[1]
    n_src = n_tgt * (ns // BLK)
    per_req = requests.shape[1]
    slots = n_clus * per_req
    width = -(-max(slots, pair_src.shape[0]) // LANES) * LANES
    asked = requests.T
    small = pltpu.CompilerParams(vmem_limit_bytes=MAIN_VMEM)
    clus_me = lax.axis_index("clus")
    me = jnp.stack([lax.axis_index("tgt"), clus_me // inner, clus_me % inner, pair_count[0]]).astype(jnp.int32)
    src_side = (src_pos, src_weight.reshape(1, -1), src_pot.reshape(1, -1))
    tgt_side = (tgt_pos, tgt_weight.reshape(1, -1), tgt_pot.reshape(1, -1))

    src_pack, tgt_pack = pl.pallas_call(
        pack_kernel,
        name="pack",
        out_shape=(jax.ShapeDtypeStruct((4, ns), f32), jax.ShapeDtypeStruct((4, nt + width), f32)),
        in_specs=[SMEM] * 3 + [VMEM] * 8,
        out_specs=(VMEM, VMEM),
        compiler_params=pltpu.CompilerParams(vmem_limit_bytes=PACK_VMEM),
    )(asked, src_count, tgt_count, pair_src.reshape(1, -1), pair_slot.reshape(1, -1), *src_side, *tgt_side)

    src_in = [src_pack] + [moved(src_pack, "tgt", k) for k in range(1, n_tgt)]
    near = [tgt_pack] + [moved_inner(tgt_pack, "clus", k) for k in range(1, inner)]
    near = pl.pallas_call(
        join_kernel,
        name="join",
        out_shape=jax.ShapeDtypeStruct((4 * inner, nt + width), f32),
        in_specs=[VMEM] * inner,
        out_specs=VMEM,
        compiler_params=small,
    )(*near)
    tgt_in = [near] + [moved_outer(near, "clus", k) for k in range(1, outer)]

    block_rows = jax.ShapeDtypeStruct((n_src + 1, 8, BLK), f32)
    left_side = jax.ShapeDtypeStruct((n_src + 1, 32, BLK), jnp.bfloat16)
    n_pairs = pair_src.shape[0]
    memo_rows = jax.ShapeDtypeStruct((len(stages(outer)) * (1 + 2 * n_pairs) + slots, LANES), jnp.int32)
    list_scratch = (
        [pltpu.SMEM((n_pairs + 1,), jnp.int32)] * 2
        + [pltpu.SemaphoreType.DMA, pltpu.SMEM(me.shape, jnp.int32)]
        + [pltpu.VMEM((4, width), jnp.int32)]
    )
    kern_bufs = [pltpu.VMEM((GROUP, 2, BLK, BLK), jnp.bfloat16)] * BUFS
    part_shape = jax.ShapeDtypeStruct((inner, 4, per_req * BLK), f32)
    state, sums = (), {}
    for turn, (first, stop) in enumerate(stages(outer)):
        begins, ends = turn == 0, turn == len(stages(outer)) - 1
        held = [k for cut in stages(outer)[1:turn] for k in range(*cut)] if ends else []
        args = ([me] + src_in if begins else list(state)) + tgt_in[first:stop] + [sums[k] for k in held]
        outs = [memo_rows, left_side, block_rows] if begins and not ends else []
        outs += [jax.ShapeDtypeStruct((4, ns), f32)] * n_tgt if ends else [block_rows]
        outs += [part_shape] * (stop - first + len(held))
        extra = [pltpu.VMEM(block_rows.shape, f32)] if ends else []
        if begins and ends:
            extra += [pltpu.VMEM(memo_rows.shape, jnp.int32)]
            extra += [pltpu.VMEM(left_side.shape, jnp.bfloat16), pltpu.VMEM(block_rows.shape, f32)]
        near = (stop - first) * inner * per_req
        extra += [
            pltpu.VMEM((near, BLK, 32), jnp.bfloat16),
            pltpu.VMEM((near, 8, BLK), f32),
            pltpu.VMEM((near, 8, BLK), f32),
        ]
        res = pl.pallas_call(
            functools.partial(pairs_kernel, n_tgt, n_clus, per_req, turn),
            name=f"pairs_{first}_{stop}",
            out_shape=outs,
            in_specs=[ANY if begins and a is me else VMEM for a in args],
            out_specs=[VMEM] * len(outs),
            scratch_shapes=extra + (list_scratch if begins else []) + kern_bufs,
            compiler_params=small,
            cost_estimate=pl.CostEstimate(flops=4*10**8 if begins else 0, bytes_accessed=2**20, transcendentals=0),
        )(*args)
        made = list(range(first, stop)) + held
        sums.update(zip(made, res[len(res) - len(made) :]))
        if ends:
            src_out = res[:n_tgt]
        else:
            state = tuple(res[:4]) if begins else state[:3] + (res[0],)

    src_parts = [src_out[0]] + [moved(src_out[k], "tgt", k) for k in range(1, n_tgt)]
    tgt_parts = [sums[0]] + [moved_outer(sums[k], "clus", flip(k, outer)) for k in range(1, outer)]
    part_keep = functools.partial(
        pl.pallas_call,
        keep_kernel,
        name="keep",
        out_shape=part_shape,
        out_specs=VMEM,
        compiler_params=small,
    )
    for k in reversed(range(2, outer)):
        late = tgt_parts[k + 1 : k + 2]
        tgt_parts[k] = part_keep(in_specs=[VMEM] * (1 + len(late)))(tgt_parts[k], *late)
    if inner == 2:
        beside = pl.pallas_call(
            pick_kernel,
            name="pick",
            out_shape=jax.ShapeDtypeStruct((outer, 4, per_req * BLK), f32),
            in_specs=[VMEM] * outer,
            out_specs=VMEM,
            compiler_params=small,
        )(*tgt_parts)
        tgt_parts.append(moved_inner(beside, "clus", 1))

    grad_src_pos, grad_src_weight, ids, live = pl.pallas_call(
        functools.partial(src_kernel, n_tgt, per_req),
        name="finish_src",
        out_shape=(
            jax.ShapeDtypeStruct((3, ns), f32),
            jax.ShapeDtypeStruct((1, ns), f32),
            jax.ShapeDtypeStruct((slots, 4, BLK), f32),
            jax.ShapeDtypeStruct((1, nt), f32),
        ),
        in_specs=[SMEM] * 3 + [VMEM] * (3 + n_tgt + outer),
        out_specs=(VMEM,) * 4,
        compiler_params=small,
    )(me, src_count, tgt_count, *src_side, *src_parts, *tgt_in)
    grad_tgt_pos, grad_tgt_weight = pl.pallas_call(
        functools.partial(tgt_kernel, outer, inner),
        name="finish_tgt",
        out_shape=(jax.ShapeDtypeStruct((3, nt), f32), jax.ShapeDtypeStruct((1, nt), f32)),
        in_specs=[VMEM] * (5 + len(tgt_parts)),
        out_specs=(VMEM,) * 2,
        compiler_params=small,
    )(*tgt_side, live, ids, *tgt_parts)
    return grad_src_pos, grad_src_weight.reshape(-1), grad_tgt_pos, grad_tgt_weight.reshape(-1)


def solution(mesh):
    placed = (
        P(None, ("clus", "tgt")),
        P(("clus", "tgt")),
        P(("clus", "tgt")),
        P(("clus", "tgt")),
        P(None, ("clus", "tgt")),
        P(("clus", "tgt")),
        P(("clus", "tgt")),
        P(("clus", "tgt")),
        P(("clus", "tgt"), None),
        P(("clus", "tgt")),
        P(("clus", "tgt")),
        P(("clus", "tgt")),
    )
    return jax.shard_map(
        shards,
        mesh=mesh,
        in_specs=placed,
        out_specs=(
            P(None, ("clus", "tgt")),
            P(("clus", "tgt")),
            P(None, ("clus", "tgt")),
            P(("clus", "tgt")),
        ),
        check_vma=False,
    )
```
